128 devices in a mesh: pts: 16 (over z, y_hi, core), grp: 8 (over x, y_lo).
Axes of the slice: x: 4, y: 4 (y_hi: 2, y_lo: 2; y = y_hi * 2 + y_lo), z: 4, core: 2. Of those that a mesh axis runs over, the one named last changes fastest.
Arguments:
- adjoint_in: bfloat16 [1152, 1280, 256], P(None, ('pts', 'grp')), may hold values from -6 to 6
- land_sea: int32 [1280, 256], P(('pts', 'grp')), may hold values 0 or 1
- depth_class: int32 [1280, 256], P(('pts', 'grp')), may hold values from 0 to 7
- damping: float32 [1280, 256], P(('pts', 'grp')), may hold values from 0.05 to 0.5
- transparency: float32 [1280, 256], P(('pts', 'grp')), may hold values from 0.6 to 1
- outlets: int32 [64], replicated, may hold values from 0 to 327679
- flux_weight: float32 [1152], replicated, may hold values from 0.5 to 2
- jacobian: bfloat16 [1152, 1152], replicated, may hold values from -0.1875 to 0.1875
- source_scale: float32 [8], replicated, may hold values from 0.1 to 0.5
- freq_damp: float32 [1152], replicated, may hold values from 0.2 to 1
- courant: float32 [32], replicated, may hold values from 0.3 to 0.45
- wind_growth: float32 [1152], replicated, may hold values from 0.01 to 0.06
Outputs:
- adjoint_out: bfloat16 [1152, 1280, 256], P(None, ('pts', 'grp'))
- wind_sens: float32 [2, 1280, 256], P(None, ('pts', 'grp'))
The draws below stay inside these ranges and needn't reach their ends.
All inputs are finite; a program needn't handle non-finite values. No bound on the sum of `land_sea` on one device may be relied on, other than what follows from the above.
Results may differ from the reference program's by a relative error of at most 0.0057.
Values may be sent and summed in bfloat16 or wider, within the bound.
No kernel may reach another device: no remote copies, remote signals or barrier semaphores. Data moves between devices by JAX's collectives and lax.ppermute only.
A program may use at most 128 MiB of HBM per device.

```python
import math
import jax
import jax.numpy as jnp
from jax import lax

DIR = 36
FREQ = 32
LON = 256
ROWS = 10
NSUB = 4
NCLASS = 8
NOUT = 64
K = 1152
LAT = 1280


def draw_adjoint_in(key, part):
    key = jax.random.fold_in(key, 11)
    value_key, start_key = jax.random.split(key, 2)
    values = jax.random.truncated_normal(value_key, -6.0, 6.0, (K, LAT, LON), jnp.float32)
    starts = jax.random.randint(start_key, (LAT, 1), 0, LON - 7, dtype=jnp.int32)
    columns = jnp.arange(LON, dtype=jnp.int32)[None, :]
    quiet = (columns >= starts) & (columns < starts + 8)
    return jnp.where(quiet[None, :, :], 0.0, values).astype(jnp.bfloat16)


def touch_ends(entries, rng, low, largest):
    extent = entries.shape
    spot = [jax.random.randint(jax.random.fold_in(rng, axis), (), 0, extent[axis]) for axis in range(len(extent))]
    entries = entries.at[tuple(spot)].set(low)
    longest = extent.index(max(extent))
    spot[longest] = (spot[longest] + 1) % extent[longest]
    return entries.at[tuple(spot)].set(largest)


def block_scale(stream_key, shape, shards, low, high):
    factor_of, own = 1.0, jax.random.fold_in(stream_key, 6)
    for axis_at, shards_of in shards:
        draws = jnp.exp(jax.random.uniform(jax.random.fold_in(own, axis_at), (shards_of,), jnp.float32, low / len(shards), high / len(shards)))
        factor_of = factor_of * jnp.repeat(draws, shape[axis_at] // shards_of).reshape([-1 if axis == axis_at else 1 for axis in range(len(shape))])
    return factor_of


def noise(key, dims, width, limit, held_as=jnp.bfloat16):
    return jnp.clip(width * jax.random.normal(key, dims, jnp.float32), -limit, limit).astype(held_as)


def setup_inputs(seed: int = 0) -> dict:
    seeds = jax.random.split(jax.random.key(seed), 13)
    return {
        "adjoint_in": draw_adjoint_in(jax.random.fold_in(seeds[12], 71), 0),
        "land_sea": touch_ends((jax.random.randint(seeds[1], (LAT, LON), 0, 10) < 7).astype(jnp.int32), jax.random.fold_in(seeds[1], 1), 0, 1),
        "depth_class": touch_ends(jax.random.randint(seeds[2], (LAT, LON), 0, NCLASS), jax.random.fold_in(seeds[2], 1), 0, NCLASS - 1).astype(jnp.int32),
        "damping": jnp.clip(jnp.exp(math.log(0.5) - 2.3025851 * jax.random.uniform(seeds[3], (LAT, LON), jnp.float32) ** block_scale(seeds[3], (LAT, LON), ((0, 128),), -0.2, 0.2)), 0.05, 0.5),
        "transparency": jnp.clip(0.6 + 0.39999998 * jax.random.uniform(seeds[4], (LAT, LON), jnp.float32) ** block_scale(seeds[4], (LAT, LON), ((0, 128),), -0.2, 0.2), 0.6, 1.0),
        "outlets": touch_ends(jax.random.randint(seeds[5], (NOUT,), 0, LAT * LON), jax.random.fold_in(seeds[5], 1), 0, (LAT * LON) - 1).astype(jnp.int32),
        "flux_weight": jnp.clip(jnp.exp(jax.random.uniform(seeds[6], (K,), jnp.float32, math.log(0.5), math.log(2.0))), 0.5, 2.0),
        "jacobian": noise(seeds[7], (K, K), K ** -0.5, 0.1875),
        "source_scale": jnp.clip(jnp.exp(jax.random.uniform(seeds[8], (NCLASS,), jnp.float32, math.log(0.1), math.log(0.5))), 0.1, 0.5),
        "freq_damp": jnp.clip(jnp.exp(jax.random.uniform(seeds[9], (K,), jnp.float32, math.log(0.2), math.log(1.0))), 0.2, 1.0),
        "courant": jnp.clip(jax.random.uniform(seeds[10], (FREQ,), jnp.float32, 0.3, 0.45), 0.3, 0.45),
        "wind_growth": jnp.clip(jnp.exp(jax.random.uniform(seeds[11], (K,), jnp.float32, math.log(0.01), math.log(0.06))), 0.01, 0.06),
    }


def direction_cosines():
    angles = 2.0 * math.pi * (jnp.arange(DIR, dtype=jnp.float32) + 0.5) / DIR
    return jnp.tile(jnp.cos(angles), FREQ), jnp.tile(jnp.sin(angles), FREQ)


def upwind_weights(courant):
    cosine, sine = direction_cosines()
    speed = jnp.repeat(courant, DIR)
    along_x = speed * cosine
    along_y = speed * sine
    zeros = jnp.zeros_like(along_x)
    return (jnp.maximum(along_x, zeros), jnp.maximum(-along_x, zeros), jnp.maximum(along_y, zeros), jnp.maximum(-along_y, zeros), 1.0 - jnp.abs(along_x) - jnp.abs(along_y))


def propagate(spectrum, weights, passage):
    eastward, westward, northward, southward, centre_keep = tuple(piece[:, None, None] for piece in weights)
    for substep in range(NSUB):
        padded = jnp.pad(spectrum, ((0, 0), (1, 1), (1, 1)))
        spectrum = passage * (centre_keep * spectrum + eastward * padded[:, 1:-1, 2:] + westward * padded[:, 1:-1, :-2] + northward * padded[:, 2:, 1:-1] + southward * padded[:, :-2, 1:-1])
    return spectrum


def source_adjoint(spectrum, jacobian, source_rate, damp_rows, freq_damp):
    coupled = jnp.dot(jacobian.T, spectrum, preferred_element_type=jnp.float32)
    values = spectrum.astype(jnp.float32)
    return (values + source_rate[None, :] * coupled - (damp_rows[None, :] * freq_damp[:, None]) * values).astype(jnp.bfloat16)


def reference(adjoint_in, land_sea, depth_class, damping, transparency, outlets, flux_weight, jacobian, source_scale, freq_damp, courant, wind_growth):
    cosine, sine = direction_cosines()
    forcing = jnp.stack([wind_growth * cosine, wind_growth * sine])
    ocean = land_sea.astype(jnp.float32)
    passage = ocean * transparency
    source_rate = source_scale[depth_class]
    flat_index = jnp.arange(LAT * LON, dtype=jnp.int32).reshape(LAT, LON)

    def count_outlet(index, total):
        return total + (flat_index == outlets[index]).astype(jnp.float32)

    seed_count = lax.fori_loop(0, NOUT, count_outlet, jnp.zeros((LAT, LON), jnp.float32))
    block_points = ROWS * LON

    def rows_of(array, row_start):
        return lax.dynamic_slice_in_dim(array, row_start, ROWS, 0).reshape(block_points)

    def first_half(block, carry):
        regrouped, wind_total = carry
        row_start = (block * ROWS).astype(jnp.int32)
        incoming = lax.dynamic_slice_in_dim(adjoint_in, row_start, ROWS, 1).reshape(K, block_points)
        seeded = (rows_of(ocean, row_start)[None, :] * (incoming.astype(jnp.float32) + flux_weight[:, None] * rows_of(seed_count, row_start)[None, :])).astype(jnp.bfloat16)
        mixed = source_adjoint(seeded, jacobian, rows_of(source_rate, row_start), rows_of(damping, row_start), freq_damp)
        wind_part = jnp.dot(forcing, seeded.astype(jnp.float32), precision=lax.Precision.HIGHEST)
        regrouped = lax.dynamic_update_slice_in_dim(regrouped, mixed.reshape(K, ROWS, LON), row_start, 1)
        wind_total = lax.dynamic_update_slice_in_dim(wind_total, wind_part.reshape(2, ROWS, LON), row_start, 1)
        return regrouped, wind_total

    regrouped, wind_total = lax.fori_loop(0, LAT // ROWS, first_half, (jnp.zeros((K, LAT, LON), jnp.bfloat16), jnp.zeros((2, LAT, LON), jnp.float32)))
    weights = upwind_weights(courant)

    def sweep(band):
        offset = (band * DIR).astype(jnp.int32)
        spectrum = lax.dynamic_slice_in_dim(regrouped, offset, DIR, 0).astype(jnp.float32)
        local = tuple(lax.dynamic_slice_in_dim(piece, offset, DIR, 0) for piece in weights)
        return propagate(spectrum, local, passage).astype(jnp.bfloat16)

    propagated = lax.map(sweep, jnp.arange(FREQ, dtype=jnp.int32)).reshape(K, LAT, LON)

    def second_half(block, carry):
        adjoint_out, wind_sens = carry
        row_start = (block * ROWS).astype(jnp.int32)
        arrived = lax.dynamic_slice_in_dim(propagated, row_start, ROWS, 1).reshape(K, block_points)
        mixed = source_adjoint(arrived, jacobian, rows_of(source_rate, row_start), rows_of(damping, row_start), freq_damp)
        wind_part = jnp.dot(forcing, arrived.astype(jnp.float32), precision=lax.Precision.HIGHEST).reshape(2, ROWS, LON)
        previous = lax.dynamic_slice_in_dim(wind_sens, row_start, ROWS, 1)
        adjoint_out = lax.dynamic_update_slice_in_dim(adjoint_out, mixed.reshape(K, ROWS, LON), row_start, 1)
        wind_sens = lax.dynamic_update_slice_in_dim(wind_sens, previous + wind_part, row_start, 1)
        return adjoint_out, wind_sens

    adjoint_out, wind_sens = lax.fori_loop(0, LAT // ROWS, second_half, (jnp.zeros((K, LAT, LON), jnp.bfloat16), wind_total))
    return adjoint_out, wind_sens
```

```python
import math

import jax
import jax.numpy as jnp
import numpy as np
from jax import lax
from jax.experimental import pallas as pl
from jax.experimental.pallas import tpu as pltpu
from jax.sharding import PartitionSpec as P

DIR = 36
FREQ = 32
NSUB = 4
NCLASS = 8
LON = 256
K = DIR * FREQ
HALF = K // 2
QUAD = K // 4
ROWS = 10
HALO = NSUB
TAIL = 16
AXES = ("pts", "grp")
VMEM = 56 * 1024 * 1024

ANGLES = 2.0 * math.pi * (np.arange(DIR) + 0.5) / DIR


def params():
    return pltpu.CompilerParams(vmem_limit_bytes=VMEM)


def whole(shape):
    return pl.BlockSpec(shape, lambda *_: (0,) * len(shape))


def three_pieces(x):
    hi = x.astype(jnp.bfloat16)
    rest = x - hi.astype(jnp.float32)
    mid = rest.astype(jnp.bfloat16)
    return hi, mid, (rest - mid.astype(jnp.float32)).astype(jnp.bfloat16)


def one_hot_order(chunk, size):
    row = lax.broadcasted_iota(jnp.int32, (size, K), 0) + chunk * size
    source = (row & (FREQ - 1)) * DIR + (row >> 5)
    column = lax.broadcasted_iota(jnp.int32, (size, K), 1)
    return jnp.where(column == source, 1.0, 0.0).astype(jnp.bfloat16)


def turn_kernel(jac_ref, out_ref):
    pick = one_hot_order(pl.program_id(0), 128)
    out_ref[...] = lax.dot_general(
        pick, jac_ref[...], (((1,), (1,)), ((), ())), preferred_element_type=jnp.float32
    ).astype(jnp.bfloat16)


def turn(jacobian):
    return pl.pallas_call(
        turn_kernel,
        grid=(K // 128,),
        in_specs=[whole((K, K))],
        out_specs=pl.BlockSpec((128, K), lambda m: (m, 0)),
        out_shape=jax.ShapeDtypeStruct((K, K), jnp.bfloat16),
        compiler_params=params(),
        cost_estimate=pl.CostEstimate(flops=2 * K**3, bytes_accessed=4 * K * K, transcendentals=0),
    )(jacobian)


def sort_columns_kernel(mat_ref, out_ref):
    pick = one_hot_order(pl.program_id(0), 128)
    out_ref[...] = lax.dot_general(
        mat_ref[...], pick, (((1,), (1,)), ((), ())), preferred_element_type=jnp.float32
    ).astype(jnp.bfloat16)


def sort_columns(mat):
    return pl.pallas_call(
        sort_columns_kernel,
        grid=(K // 128,),
        in_specs=[whole((K, K))],
        out_specs=pl.BlockSpec((K, 128), lambda m: (0, m)),
        out_shape=jax.ShapeDtypeStruct((K, K), jnp.bfloat16),
        compiler_params=params(),
        cost_estimate=pl.CostEstimate(flops=2 * K**3, bytes_accessed=4 * K * K, transcendentals=0),
    )(mat)


def wind_rows(forcing, values):
    parts = jnp.concatenate([*three_pieces(forcing), jnp.zeros((8, K), jnp.bfloat16)], axis=0)
    sums = jnp.dot(parts, values, preferred_element_type=jnp.float32)
    return sums[0:8] + sums[8:16] + sums[16:24]


def first_kernel(half, first_row, halo, x_ref, sea_ref, count_ref, rate_ref, damp_ref, pass_ref,
                 fw_ref, fd_ref, jac_ref, forcing_ref, *rest):
    if halo:
        out_a, out_b, held = rest
    else:
        out_a, wind_ref, held = rest
    r = pl.program_id(0) + first_row
    sea = sea_ref[pl.ds(r, 1), :]
    count = count_ref[pl.ds(r, 1), :]
    rate = rate_ref[pl.ds(r, 1), :]
    damp = damp_ref[pl.ds(r, 1), :]
    fw = jnp.concatenate([fw_ref[...], fw_ref[...]], axis=1)
    seeded = (sea * (x_ref[0].astype(jnp.float32) + fw * count)).astype(jnp.bfloat16)
    values = seeded.astype(jnp.float32)
    held[0] = values[:, :128]
    held[1] = values[:, 128:]
    for m in range(HALF // 64):
        rows = slice(m * 64, (m + 1) * 64)
        mixed = jnp.dot(jac_ref[rows, :], seeded, preferred_element_type=jnp.float32)
        fd = fd_ref[rows, :]
        for side in range(2):
            lanes = slice(side * 128, (side + 1) * 128)
            d = half * 18 + 2 * m
            v = jnp.concatenate(
                [held[side, pl.ds(d + e, FREQ, stride=DIR), :] for e in range(2)], axis=0
            )
            moved = v + rate[:, lanes] * mixed[:, lanes] - (damp[:, lanes] * fd) * v
            moved = moved.astype(jnp.bfloat16)
            if not halo:
                out_a[0, rows, lanes] = moved
            elif m * 64 + 64 <= QUAD:
                out_a[0, rows, lanes] = moved
            elif m * 64 >= QUAD:
                out_b[0, m * 64 - QUAD : m * 64 - QUAD + 64, lanes] = moved
            else:
                out_a[0, m * 64 : m * 64 + 32, lanes] = moved[:32]
                out_b[0, 0:32, lanes] = moved[32:]
    if halo:
        pieces = [jnp.broadcast_to(p, (8, LON)).astype(jnp.float32)
                  for p in three_pieces(pass_ref[pl.ds(r, 1), :])]
        which = lax.broadcasted_iota(jnp.int32, (8, LON), 0)
        tail = jnp.where(which == 0, pieces[0], jnp.where(which == 1, pieces[1], jnp.where(which == 2, pieces[2], 0.0)))
        out_a[0, QUAD : QUAD + TAIL, :] = jnp.concatenate([tail, jnp.zeros((8, LON), jnp.float32)], axis=0).astype(jnp.bfloat16)
    else:
        wind_ref[0] = wind_rows(forcing_ref[...], seeded)


def first_source(half, first_row, count_rows, halo, x, sea, count, rate, damp, passage, fw, fd, jac, forcing):
    point = whole((ROWS, LON))
    if halo:
        shapes = [(count_rows, QUAD + TAIL, LON), (count_rows, QUAD, LON)]
        out_shape = [jax.ShapeDtypeStruct(s, jnp.bfloat16) for s in shapes]
    else:
        shapes = [(count_rows, HALF, LON), (count_rows, 8, LON)]
        out_shape = [jax.ShapeDtypeStruct(shapes[0], jnp.bfloat16), jax.ShapeDtypeStruct(shapes[1], jnp.float32)]

    def body(*refs):
        first_kernel(half, first_row, halo, *refs)

    return pl.pallas_call(
        body,
        grid=(count_rows,),
        in_specs=[
            pl.BlockSpec((1, K, LON), lambda i: (i + first_row, 0, 0)),
            point, point, point, point, point,
            whole((K, 128)),
            pl.BlockSpec((HALF, 128), lambda i: (half, 0)),
            pl.BlockSpec((HALF, K), lambda i: (half, 0)),
            whole((8, K)),
        ],
        out_specs=[pl.BlockSpec((1, *s[1:]), lambda i: (i, 0, 0)) for s in shapes],
        out_shape=out_shape,
        scratch_shapes=[pltpu.VMEM((2, K, 128), jnp.float32)],
        compiler_params=params(),
        cost_estimate=pl.CostEstimate(
            flops=2 * K * HALF * LON * count_rows, bytes_accessed=4 * K * LON * count_rows, transcendentals=0
        ),
    )(x, sea, count, rate, damp, passage, fw, fd, jac, forcing)


def sweep_kernel(quad, table_ref, own_pass_ref, halo_pass_ref, courant_ref, edge_ref, inner_ref, halo_ref,
                 out_ref, pass_rows):
    north = quad < 2
    east = quad in (0, 3)
    d = pl.program_id(0)

    @pl.when(d == 0)
    def _():
        for t in range(ROWS + HALO - 1):
            if t < ROWS:
                own = t if north else ROWS - 1 - t
                row = own_pass_ref[own : own + 1, :]
            else:
                far = t - ROWS if north else HALO - 1 - (t - ROWS)
                pieces = halo_pass_ref[far].astype(jnp.float32)
                row = pieces[0:1] + pieces[1:2] + pieces[2:3]
            pass_rows[t] = jnp.broadcast_to(row, (8, LON))

    along_x = table_ref[0, d]
    along_y = table_ref[1, d]
    lane = lax.broadcasted_iota(jnp.int32, (8, LON), 1)
    inside = lane < LON - 1 if east else lane > 0
    for group in range(2):
        rows = slice(group * 16, (group + 1) * 16)
        blocks = []
        for t in range(ROWS + HALO):
            if north:
                ref, at = (edge_ref, t) if t < 4 else (inner_ref, t - 4) if t < 10 else (halo_ref, t - 10)
            else:
                ref, at = (edge_ref, 3 - t) if t < 4 else (inner_ref, 9 - t) if t < 10 else (halo_ref, 13 - t)
            blocks.append(ref[at, rows, :].astype(jnp.float32))
        done = []
        for part in range(2):
            speed = courant_ref[group * 16 + part * 8 : group * 16 + part * 8 + 8, :]
            speed = jnp.concatenate([speed, speed], axis=1)
            across = speed * along_x
            upward = speed * along_y
            centre = 1.0 - across - upward
            across = jnp.where(inside, across, 0.0)
            v = [b[part * 8 : part * 8 + 8] for b in blocks]
            for step in range(NSUB):
                v = [
                    pass_rows[t]
                    * (centre * v[t] + across * pltpu.roll(v[t], LON - 1 if east else 1, 1) + upward * v[t + 1])
                    for t in range(len(v) - 1)
                ]
            done.append(v)
        for t in range(ROWS):
            out_ref[t if north else ROWS - 1 - t, rows, :] = jnp.concatenate(
                [done[0][t], done[1][t]], axis=0
            ).astype(jnp.bfloat16)


def sweep(quad, table, passage, carrier, courant, edge, inner, halo):
    def body(*refs):
        sweep_kernel(quad, *refs)

    inner_at = (quad % 2) * (QUAD // FREQ)
    return pl.pallas_call(
        body,
        grid=(QUAD // FREQ,),
        in_specs=[
            pl.BlockSpec(memory_space=pltpu.SMEM),
            whole((ROWS, LON)),
            pl.BlockSpec((HALO, TAIL, LON), lambda d: (0, QUAD // TAIL, 0)),
            whole((FREQ, 128)),
            pl.BlockSpec((HALO, FREQ, LON), lambda d: (0, d, 0)),
            pl.BlockSpec((ROWS - HALO, FREQ, LON), lambda d: (0, d + inner_at, 0)),
            pl.BlockSpec((HALO, FREQ, LON), lambda d: (0, d, 0)),
        ],
        out_specs=pl.BlockSpec((ROWS, FREQ, LON), lambda d: (0, d, 0)),
        out_shape=jax.ShapeDtypeStruct((ROWS, QUAD, LON), jnp.bfloat16),
        scratch_shapes=[pltpu.VMEM((ROWS + HALO - 1, 8, LON), jnp.float32)],
        compiler_params=params(),
        cost_estimate=pl.CostEstimate(
            flops=46 * 7 * QUAD * LON, bytes_accessed=48 * QUAD * LON, transcendentals=0
        ),
    )(table, passage, carrier, courant, edge, inner, halo)


def second_kernel(v0, v1, v2, v3, rate_ref, damp_ref, fd_ref, jac_ref, forcing_ref, wind_in, out_ref, wind_ref,
                  joined, held):
    r = pl.program_id(0)
    rate = rate_ref[pl.ds(r, 1), :]
    damp = damp_ref[pl.ds(r, 1), :]
    for q, v_ref in enumerate((v0, v1, v2, v3)):
        joined[q * QUAD : (q + 1) * QUAD, :] = v_ref[0]
    spectrum = joined[...]
    for m in range(K // 64):
        rows = slice(m * 64, (m + 1) * 64)
        mixed = jnp.dot(jac_ref[rows, :], spectrum, preferred_element_type=jnp.float32)
        fd = fd_ref[rows, :]
        for side in range(2):
            lanes = slice(side * 128, (side + 1) * 128)
            v = joined[rows, lanes].astype(jnp.float32)
            moved = v + rate[:, lanes] * mixed[:, lanes] - (damp[:, lanes] * fd) * v
            for e in range(2):
                held[side, pl.ds(2 * m + e, FREQ, stride=DIR), :] = moved[e * FREQ : (e + 1) * FREQ]
    for side in range(2):
        out_ref[0, :, side * 128 : (side + 1) * 128] = held[side].astype(jnp.bfloat16)
    wind_ref[0] = wind_in[0] + wind_rows(forcing_ref[...], spectrum)


def second_source(swept, rate, damp, fd, jac, forcing, wind):
    point = whole((ROWS, LON))
    return pl.pallas_call(
        second_kernel,
        grid=(ROWS,),
        in_specs=[pl.BlockSpec((1, QUAD, LON), lambda r: (r, 0, 0))] * 4
        + [
            point, point,
            whole((K, 128)),
            whole((K, K)),
            whole((8, K)),
            pl.BlockSpec((1, 8, LON), lambda r: (r, 0, 0)),
        ],
        out_specs=[
            pl.BlockSpec((1, K, LON), lambda r: (r, 0, 0)),
            pl.BlockSpec((1, 8, LON), lambda r: (r, 0, 0)),
        ],
        out_shape=[
            jax.ShapeDtypeStruct((ROWS, K, LON), jnp.bfloat16),
            jax.ShapeDtypeStruct((ROWS, 8, LON), jnp.float32),
        ],
        scratch_shapes=[pltpu.VMEM((K, LON), jnp.bfloat16), pltpu.VMEM((2, K, 128), jnp.float32)],
        compiler_params=params(),
        cost_estimate=pl.CostEstimate(
            flops=2 * K * K * LON * ROWS, bytes_accessed=4 * K * LON * ROWS, transcendentals=0
        ),
    )(*swept, rate, damp, fd, jac, forcing, wind)


def by_direction(per_component):
    return per_component.reshape(FREQ, DIR).T.reshape(K)


def body(
    adjoint_in,
    land_sea,
    depth_class,
    damping,
    transparency,
    outlets,
    flux_weight,
    jacobian,
    source_scale,
    freq_damp,
    courant,
    wind_growth,
):
    devices = lax.axis_size(AXES)
    position = lax.axis_index(AXES)
    x = adjoint_in.transpose(1, 0, 2)
    sea = land_sea.astype(jnp.float32)
    passage = sea * transparency
    rate = jnp.zeros((ROWS, LON), jnp.float32)
    for c in range(NCLASS):
        rate = jnp.where(depth_class == c, source_scale[c], rate)
    flat = (
        position * (ROWS * LON)
        + lax.broadcasted_iota(jnp.int32, (ROWS, LON), 0) * LON
        + lax.broadcasted_iota(jnp.int32, (ROWS, LON), 1)
    )
    count = jnp.sum((flat[None] == outlets[:, None, None]).astype(jnp.float32), axis=0)
    cosine = jnp.asarray(np.tile(np.cos(ANGLES), FREQ), jnp.float32)
    sine = jnp.asarray(np.tile(np.sin(ANGLES), FREQ), jnp.float32)
    forcing = jnp.pad(jnp.stack([wind_growth * cosine, wind_growth * sine]), ((0, 6), (0, 0)))
    forcing_sorted = forcing.reshape(8, FREQ, DIR).transpose(0, 2, 1).reshape(8, K)
    fw = jnp.broadcast_to(flux_weight[:, None], (K, 128))
    fd = jnp.broadcast_to(by_direction(freq_damp)[:, None], (K, 128))
    speed = jnp.broadcast_to(courant[:, None], (FREQ, 128))

    turned = turn(jacobian)
    common = (x, sea, count, rate, damping, passage, fw, fd, turned, forcing)
    down = [(i + 1, i) for i in range(devices - 1)]
    up = [(i, i + 1) for i in range(devices - 1)]
    south_edge = first_source(0, 0, HALO, True, *common)
    north_edge = first_source(1, ROWS - HALO, HALO, True, *common)
    edges = [south_edge[0], south_edge[1], north_edge[0], north_edge[1]]
    halos = [None] * 4
    for q in (0, 2, 1, 3):
        halos[q] = lax.ppermute(edges[q], AXES, down if q < 2 else up)
    north_inner, wind_high = first_source(0, HALO, ROWS - HALO, False, *common)
    south_inner, wind_low = first_source(1, 0, ROWS - HALO, False, *common)
    sorted_jac = sort_columns(turned)
    wind = jnp.concatenate([wind_low[:HALO], wind_high], axis=0)
    swept = [None] * 4
    per = QUAD // FREQ
    for q in (0, 2, 1, 3):
        angles = ANGLES[q * per : (q + 1) * per]
        table = jnp.asarray(np.abs(np.stack([np.cos(angles), np.sin(angles)])), jnp.float32)
        carrier = halos[0] if q < 2 else halos[2]
        inner = north_inner if q < 2 else south_inner
        swept[q] = sweep(q, table, passage, carrier, speed, edges[q], inner, halos[q])
    out, wind_out = second_source(swept, rate, damping, fd, sorted_jac, forcing_sorted, wind)
    return out.transpose(1, 0, 2), wind_out[:, :2, :].transpose(1, 0, 2)


def solution(mesh):
    rows = P(AXES, None)
    placed = (P(None, AXES, None), rows, rows, rows, rows, P(), P(), P(), P(), P(), P(), P())
    return jax.shard_map(
        body,
        mesh=mesh,
        in_specs=placed,
        out_specs=(P(None, AXES, None), P(None, AXES, None)),
        check_vma=False,
    )
```

```python
import math

import jax
import jax.numpy as jnp
import numpy as np
from jax import lax
from jax.experimental import pallas as pl
from jax.experimental.pallas import tpu as pltpu
from jax.sharding import PartitionSpec as P

DIR = 36
FREQ = 32
NSUB = 4
NCLASS = 8
LON = 256
K = DIR * FREQ
HALF = K // 2
QUAD = K // 4
ROWS = 10
HALO = NSUB
TAIL = 16
AXES = ("pts", "grp")
VMEM = 56 * 1024 * 1024

ANGLES = 2.0 * math.pi * (np.arange(DIR) + 0.5) / DIR


def params():
    return pltpu.CompilerParams(vmem_limit_bytes=VMEM)


def whole(shape):
    return pl.BlockSpec(shape, lambda *_: (0,) * len(shape))


def block(*shape):
    return pl.BlockSpec(shape, lambda i: (i,) + (0,) * (len(shape) - 1))


def smem():
    return pl.BlockSpec(memory_space=pltpu.SMEM)


def cost(flops, read):
    return pl.CostEstimate(flops=int(flops), bytes_accessed=int(read), transcendentals=0)


def three_pieces(x):
    hi = x.astype(jnp.bfloat16).astype(jnp.float32)
    mid = (x - hi).astype(jnp.bfloat16).astype(jnp.float32)
    return hi, mid, x - hi - mid


def stack_pieces(pieces):
    which = lax.broadcasted_iota(jnp.int32, (8, LON), 0)
    rows = jnp.zeros((8, LON), jnp.float32)
    for at, piece in enumerate(pieces):
        rows = jnp.where(which == at, jnp.broadcast_to(piece, (8, LON)), rows)
    return jnp.concatenate([rows, jnp.zeros((8, LON), jnp.float32)], axis=0).astype(jnp.bfloat16)


def contract(matrix, spectrum):
    return lax.dot_general(matrix, spectrum, (((0,), (0,)), ((), ())), preferred_element_type=jnp.float32)


def column(vector):
    return jnp.broadcast_to(vector, (128, K)).T


def point_fields(land_ref, depth_ref, outlets_ref, scale_ref, sea, count, rate):
    sea[...] = land_ref[...].astype(jnp.float32)
    depth = depth_ref[...]
    total = jnp.zeros((ROWS, LON), jnp.float32)
    for c in range(NCLASS):
        total = jnp.where(depth == c, scale_ref[c], total)
    rate[...] = total
    shape = (ROWS, LON)
    flat = lax.broadcasted_iota(jnp.int32, shape, 0) * LON + lax.broadcasted_iota(jnp.int32, shape, 1)
    flat = flat + lax.axis_index(AXES) * (ROWS * LON)
    hits = jnp.zeros(shape, jnp.float32)
    for n in range(outlets_ref.shape[0]):
        hits = hits + jnp.where(flat == outlets_ref[n], 1.0, 0.0)
    count[...] = hits


def first_kernel(part, x_ref, land_ref, depth_ref, damp_ref, clear_ref, outlets_ref, scale_ref,
                 comp_a, comp_b, comp_c, jac_ref, *rest):
    sea, count, rate, held = rest[-4:]
    step = pl.program_id(0)
    if part == "south":
        fw_ref, fd_ref, wave_ref, message, other, wind_ref = rest[:-4]
        first_row = 2 * step
    else:
        fw_ref, fd_ref, wave_ref = comp_a, comp_b, comp_c
        message, other, middle, wind_ref = rest[:-4]
        first_row = jnp.where(step == 2, 4, 2 * step + 6)

    @pl.when(step == 0)
    def _():
        point_fields(land_ref, depth_ref, outlets_ref, scale_ref, sea, count, rate)
        if part == "south":
            fw_ref[...] = column(comp_a[0:1, :])
            fd_ref[...] = column(comp_a[1:2, :])
            forcing = column(comp_a[2:3, :]) * comp_b[...]
            hi, mid, low = three_pieces(forcing)
            lane = lax.broadcasted_iota(jnp.int32, (K, 128), 1)
            mixed = jnp.where(lane < 8, hi, jnp.where(lane < 16, mid, low))
            wave_ref[...] = mixed.astype(jnp.bfloat16)

    fw = fw_ref[...]
    fw = jnp.concatenate([fw, fw], axis=1)
    seeds = []
    fields = []
    for e in range(2):
        r = first_row + e
        lone = sea[pl.ds(r, 1), :] * (x_ref[e].astype(jnp.float32) + fw * count[pl.ds(r, 1), :])
        seeds.append(lone.astype(jnp.bfloat16))
        fields.append((rate[pl.ds(r, 1), :], damp_ref[pl.ds(r, 1), :]))
    spectrum = jnp.concatenate(seeds, axis=1)
    for m in range(3):
        rows = slice(m * 384, (m + 1) * 384)
        mixed = contract(jac_ref[:, rows], spectrum)
        fd = fd_ref[rows, :]
        for piece in range(4):
            e, side = divmod(piece, 2)
            lanes = slice(side * 128, (side + 1) * 128)
            at = slice(piece * 128, (piece + 1) * 128)
            v = seeds[e][rows, lanes].astype(jnp.float32)
            held[piece, rows, :] = (
                v + fields[e][0][:, lanes] * mixed[:, at] - (fields[e][1][:, lanes] * fd) * v
            )
    wind = contract(wave_ref[...], spectrum)
    wind = wind[0:8] + wind[8:16] + wind[16:24]
    wind_ref[0] = wind[:, :LON]
    wind_ref[1] = wind[:, LON:]

    def half_out(half, ref):
        for d in range(18):
            for piece in range(4):
                e, side = divmod(piece, 2)
                ref[e, d * FREQ : (d + 1) * FREQ, side * 128 : (side + 1) * 128] = held[
                    piece, pl.ds(half * 18 + d, FREQ, stride=DIR), :
                ].astype(jnp.bfloat16)

    def message_out(half):
        half_out(half, message)
        for e in range(2):
            r = first_row + e
            passage = sea[pl.ds(r, 1), :] * clear_ref[pl.ds(r, 1), :]
            message[e, HALF : HALF + TAIL, :] = stack_pieces(three_pieces(passage))

    if part == "south":
        message_out(0)
        half_out(1, other)
    else:
        half_out(0, other)

        @pl.when(step < 2)
        def _():
            message_out(1)

        @pl.when(step == 2)
        def _():
            half_out(1, middle)


def first_source(part, x, land, depth, damping, clear, outlets, scale, comps, jacobian):
    point = whole((ROWS, LON))
    comp_specs = [whole(c.shape) for c in comps]
    out_specs, out_shape = [], []

    def add(spec, shape, dtype=jnp.bfloat16):
        out_specs.append(spec)
        out_shape.append(jax.ShapeDtypeStruct(shape, dtype))

    def rows_at(index, size):
        return pl.BlockSpec((2, size, LON), lambda i: (index(i), 0, 0))

    if part == "south":
        count_rows = 4
        source = rows_at(lambda i: i, K)
        for dtype in (jnp.float32, jnp.float32, jnp.bfloat16):
            add(whole((K, 128)), (K, 128), dtype)
        add(rows_at(lambda i: i, HALF + TAIL), (4, HALF + TAIL, LON))
        add(rows_at(lambda i: i, HALF), (4, HALF, LON))
        add(rows_at(lambda i: i, 8), (4, 8, LON), jnp.float32)
    else:
        count_rows = 6
        source = rows_at(lambda i: jnp.where(i == 2, 2, i + 3), K)
        add(rows_at(lambda i: jnp.minimum(i, 1), HALF + TAIL), (4, HALF + TAIL, LON))
        add(rows_at(lambda i: jnp.where(i == 2, 0, i + 1), HALF), (6, HALF, LON))
        add(rows_at(lambda i: 0, HALF), (2, HALF, LON))
        add(rows_at(lambda i: jnp.where(i == 2, 0, i + 1), 8), (6, 8, LON), jnp.float32)

    def body(*refs):
        first_kernel(part, *refs)

    return pl.pallas_call(
        body,
        grid=(count_rows // 2,),
        in_specs=[source] + [point] * 4 + [smem(), smem()] + comp_specs + [whole((K, K))],
        out_specs=out_specs,
        out_shape=out_shape,
        scratch_shapes=[pltpu.VMEM((ROWS, LON), jnp.float32)] * 3 + [pltpu.VMEM((4, K, 128), jnp.float32)],
        compiler_params=params(),
        cost_estimate=cost(0, 0),
        name="first_source_" + part,
    )(x, land, depth, damping, clear, outlets, scale, *comps, jacobian)


SPLIT = 1
PART = QUAD // SPLIT
STEPS = 4 * SPLIT


def sweep_rows(quad, table_ref, courant_ref, pass_rows, step, load, emit):
    east = quad in (0, 3)
    lane = lax.broadcasted_iota(jnp.int32, (16, 128), 1)
    last = lane == 127 if east else lane == 0
    shift = 127 if east else 1
    halves = (slice(0, 128), slice(128, 256))
    order = halves if east else halves[::-1]

    def chunk(i, carry):
        d = step * (PART // FREQ) + i // 2
        rows = pl.ds(pl.multiple_of(i * 16, 16), 16)
        speed = courant_ref[pl.ds(pl.multiple_of((i % 2) * 16, 16), 16), :]
        across = speed * table_ref[0, d]
        upward = speed * table_ref[1, d]
        centre = 1.0 - across - upward
        walled = jnp.where(last, 0.0, across)

        def advance(v, first):
            turned = [[pltpu.roll(value, shift, 1) for value in half[:-1]] for half in v]
            fresh = [[], []]
            for t in range(len(v[0]) - 1):
                beside = (jnp.where(last, turned[1][t], turned[0][t]), turned[1][t])
                for half, weight in ((0, across), (1, walled)):
                    fresh[half].append(
                        pass_rows[first + t, :, order[half]]
                        * (centre * v[half][t] + weight * beside[half] + upward * v[half][t + 1])
                    )
            return fresh

        emit(rows, order, advance)
        return carry

    lax.fori_loop(0, PART // 16, chunk, 0, unroll=3)


def own_passage(land_ref, clear_ref, pass_rows, north):
    passage = land_ref[...].astype(jnp.float32) * clear_ref[...]
    for t in range(ROWS):
        own = t if north else ROWS - 1 - t
        pass_rows[t] = jnp.broadcast_to(passage[own : own + 1, :], (16, LON))


def inner_kernel(table_ref, land_ref, clear_ref, courant_ref, low_n, high_n, low_s, mid_s, high_s,
                 done_n, state_n, done_s, state_s, pass_rows):
    step = pl.program_id(0)

    def quadrant(quad):
        north = quad < 2

        @pl.when(step == quad * SPLIT)
        def _():
            own_passage(land_ref, clear_ref, pass_rows, north)

        def load(t, rows, lanes):
            r = t if north else ROWS - 1 - t
            if north:
                value = low_n[r, rows, lanes] if r < 4 else high_n[r - 4, rows, lanes]
            else:
                value = low_s[r, rows, lanes] if r < 4 else mid_s[r - 4, rows, lanes] if r < 6 else high_s[r - 6, rows, lanes]
            return value.astype(jnp.float32)

        done, state = (done_n, state_n) if north else (done_s, state_s)

        def emit(rows, order, advance):
            v = [[load(t, rows, lanes) for t in range(ROWS)] for lanes in order]
            for s in range(NSUB):
                v = advance(v, 0)
                if s < NSUB - 1:
                    for half in range(2):
                        state[s, rows, order[half]] = v[half][-1]
            for half in range(2):
                for t in range(ROWS - NSUB):
                    done[t if north else ROWS - NSUB - 1 - t, rows, order[half]] = v[half][t].astype(jnp.bfloat16)

        @pl.when((step >= quad * SPLIT) & (step < (quad + 1) * SPLIT))
        def _():
            sweep_rows(quad, table_ref, courant_ref, pass_rows, step, load, emit)

    for quad in range(4):
        quadrant(quad)


def north_rows(count_rows, at=0):
    return pl.BlockSpec((count_rows, PART, LON), lambda i: (at, jnp.minimum(i, STEPS // 2 - 1), 0))


def south_rows(count_rows, at=0):
    return pl.BlockSpec((count_rows, PART, LON), lambda i: (at, jnp.maximum(i - STEPS // 2, 0), 0))


def inner_sweep(table, land, clear, courant, low_n, high_n, low_s, mid_s, high_s):
    return pl.pallas_call(
        inner_kernel,
        grid=(STEPS,),
        in_specs=[
            smem(), whole((ROWS, LON)), whole((ROWS, LON)), whole((FREQ, 128)),
            north_rows(4), north_rows(6), south_rows(4), south_rows(2), south_rows(4),
        ],
        out_specs=[north_rows(6), north_rows(3), south_rows(6), south_rows(3)],
        out_shape=[
            jax.ShapeDtypeStruct((6, HALF, LON), jnp.bfloat16),
            jax.ShapeDtypeStruct((3, HALF, LON), jnp.float32),
        ] * 2,
        scratch_shapes=[pltpu.VMEM((ROWS, 16, LON), jnp.float32)],
        compiler_params=params(),
        cost_estimate=cost(0, 0),
        name="inner_sweep",
    )(table, land, clear, courant, low_n, high_n, low_s, mid_s, high_s)


def outer_kernel(north, table_ref, land_ref, clear_ref, courant_ref, halo_pass, first, state, halo, done, pass_rows):
    step = pl.program_id(0)

    @pl.when(step == 0)
    def _():
        own_passage(land_ref, clear_ref, pass_rows, north)
        for t in range(HALO - 1):
            pieces = halo_pass[t if north else HALO - 1 - t].astype(jnp.float32)
            pass_rows[ROWS + t] = jnp.broadcast_to(pieces[0:1] + pieces[1:2] + pieces[2:3], (16, LON))

    def emit(rows, order, advance):
        v = [
            [first[0, rows, lanes].astype(jnp.float32)]
            + [halo[t if north else HALO - 1 - t, rows, lanes].astype(jnp.float32) for t in range(HALO)]
            for lanes in order
        ]
        for s in range(NSUB):
            v = advance(v, ROWS - 1 - s)
            if s < NSUB - 1:
                v = [[state[s, rows, lanes]] + half for lanes, half in zip(order, v)]
        for half in range(2):
            for t in range(HALO):
                done[t if north else HALO - 1 - t, rows, order[half]] = v[half][t].astype(jnp.bfloat16)

    for quad in (0, 1) if north else (2, 3):
        at = quad % 2

        @pl.when((step >= at * SPLIT) & (step < (at + 1) * SPLIT))
        def _():
            sweep_rows(quad, table_ref, courant_ref, pass_rows, step + (quad - at) * SPLIT, None, emit)


def outer_sweep(north, table, land, clear, courant, first, state, halo):
    def rows_of(count_rows, at=0):
        return pl.BlockSpec((count_rows, PART, LON), lambda i: (at, i, 0))

    def body(*refs):
        outer_kernel(north, *refs)

    return pl.pallas_call(
        body,
        grid=(STEPS // 2,),
        in_specs=[
            smem(), whole((ROWS, LON)), whole((ROWS, LON)), whole((FREQ, 128)),
            pl.BlockSpec((HALO, TAIL, LON), lambda i: (0, HALF // TAIL, 0)),
            rows_of(1, 5 if north else 0), rows_of(3), rows_of(4),
        ],
        out_specs=rows_of(4),
        out_shape=jax.ShapeDtypeStruct((4, HALF, LON), jnp.bfloat16),
        scratch_shapes=[pltpu.VMEM((ROWS + HALO - 1, 16, LON), jnp.float32)],
        compiler_params=params(),
        cost_estimate=cost(16 * 7 * K * LON * 40, 50 * K * LON),
        name="outer_sweep_north" if north else "outer_sweep_south",
    )(table, land, clear, courant, halo, first, state, halo)


def second_kernel(in_n, out_n, in_s, out_s, land_ref, depth_ref, damp_ref, scale_ref, fd_ref, jac_ref, wave_ref,
                  wind_a, wind_b, out_ref, wind_ref, rate, held):
    step = pl.program_id(0)

    @pl.when(step == 0)
    def _():
        depth = depth_ref[...]
        total = jnp.zeros((ROWS, LON), jnp.float32)
        for c in range(NCLASS):
            total = jnp.where(depth == c, scale_ref[c], total)
        rate[...] = total

    def take(half, ref):
        for d in range(18):
            for piece in range(4):
                e, side = divmod(piece, 2)
                held[piece, pl.ds(half * 18 + d, FREQ, stride=DIR), :] = ref[
                    e, d * FREQ : (d + 1) * FREQ, side * 128 : (side + 1) * 128
                ].astype(jnp.float32)

    pl.when(step < 3)(lambda: take(0, in_n))
    pl.when(step >= 3)(lambda: take(0, out_n))
    pl.when(step < 2)(lambda: take(1, out_s))
    pl.when(step >= 2)(lambda: take(1, in_s))
    spectrum = jnp.concatenate([held[piece].astype(jnp.bfloat16) for piece in range(4)], axis=1)
    fields = []
    for e in range(2):
        r = 2 * step + e
        fields.append((rate[pl.ds(r, 1), :], damp_ref[pl.ds(r, 1), :]))
    for m in range(3):
        rows = slice(m * 384, (m + 1) * 384)
        mixed = contract(jac_ref[:, rows], spectrum)
        fd = fd_ref[rows, :]
        for piece in range(4):
            e, side = divmod(piece, 2)
            lanes = slice(side * 128, (side + 1) * 128)
            at = slice(piece * 128, (piece + 1) * 128)
            v = held[piece, rows, :]
            out_ref[e, rows, lanes] = (
                v + fields[e][0][:, lanes] * mixed[:, at] - (fields[e][1][:, lanes] * fd) * v
            ).astype(jnp.bfloat16)
    wind = contract(wave_ref[...], spectrum)
    wind = wind[0:8] + wind[8:16] + wind[16:24]
    for e in range(2):
        before = jnp.where(step < 2, wind_a[e], wind_b[e])
        wind_ref[e] = (before + wind[:, e * LON : (e + 1) * LON])[:2]


def second_source(in_n, out_n, in_s, out_s, land, depth, damping, scale, fd, jac, wave, wind_low, wind_high):
    point = whole((ROWS, LON))

    def at(index, size):
        return pl.BlockSpec((2, size, LON), lambda i: (index(i), 0, 0))

    return pl.pallas_call(
        second_kernel,
        grid=(ROWS // 2,),
        in_specs=[
            at(lambda i: jnp.minimum(i, 2), HALF),
            at(lambda i: jnp.maximum(i - 3, 0), HALF),
            at(lambda i: jnp.maximum(i - 2, 0), HALF),
            at(lambda i: jnp.minimum(i, 1), HALF),
            point, point, point, smem(),
            whole((K, 128)), whole((K, K)), whole((K, 128)),
            at(lambda i: jnp.minimum(i, 1), 8),
            at(lambda i: jnp.maximum(i - 2, 0), 8),
        ],
        out_specs=[block(2, K, LON), block(2, 2, LON)],
        out_shape=[
            jax.ShapeDtypeStruct((ROWS, K, LON), jnp.bfloat16),
            jax.ShapeDtypeStruct((ROWS, 2, LON), jnp.float32),
        ],
        scratch_shapes=[pltpu.VMEM((ROWS, LON), jnp.float32), pltpu.VMEM((4, K, 128), jnp.float32)],
        compiler_params=params(),
        cost_estimate=cost(2 * K * K * LON * ROWS * 2, 4 * K * LON * ROWS),
        name="second_source",
    )(in_n, out_n, in_s, out_s, land, depth, damping, scale, fd, jac, wave, wind_low, wind_high)


def body(
    adjoint_in,
    land_sea,
    depth_class,
    damping,
    transparency,
    outlets,
    flux_weight,
    jacobian,
    source_scale,
    freq_damp,
    courant,
    wind_growth,
):
    devices = lax.axis_size(AXES)
    x = adjoint_in.transpose(1, 0, 2)
    compass = np.zeros((K, 128), np.float32)
    for at in range(3):
        compass[:, 8 * at] = np.tile(np.cos(ANGLES), FREQ)
        compass[:, 8 * at + 1] = np.tile(np.sin(ANGLES), FREQ)
    comps = (jnp.stack([flux_weight, freq_damp, wind_growth]), jnp.asarray(compass))
    common = (x, land_sea, depth_class, damping, transparency, outlets, source_scale)
    fw, fd, wave, low_n, low_s, wind_low = first_source("south", *common, comps + (comps[0],), jacobian)
    halo_n = lax.ppermute(low_n, AXES, [(i + 1, i) for i in range(devices - 1)])
    high_s, high_n, mid_s, wind_high = first_source("north", *common, (fw, fd, wave), jacobian)
    halo_s = lax.ppermute(high_s, AXES, [(i, i + 1) for i in range(devices - 1)])
    speed = jnp.broadcast_to(courant[:, None], (FREQ, 128))
    table = jnp.asarray(np.abs(np.stack([np.cos(ANGLES), np.sin(ANGLES)])), jnp.float32)
    local = (table, land_sea, transparency, speed)
    in_n, state_n, in_s, state_s = inner_sweep(*local, low_n, high_n, low_s, mid_s, high_s)
    out_n = outer_sweep(True, *local, high_n, state_n, halo_n)
    state_s, out_n = lax.optimization_barrier((state_s, out_n))
    out_s = outer_sweep(False, *local, low_s, state_s, halo_s)
    out, wind_out = second_source(
        in_n, out_n, in_s, out_s, land_sea, depth_class, damping, source_scale, fd, jacobian, wave,
        wind_low, wind_high,
    )
    return out.transpose(1, 0, 2), wind_out.transpose(1, 0, 2)


def solution(mesh):
    rows = P(AXES, None)
    placed = (P(None, AXES, None), rows, rows, rows, rows, P(), P(), P(), P(), P(), P(), P())
    return jax.shard_map(
        body,
        mesh=mesh,
        in_specs=placed,
        out_specs=(P(None, AXES, None), P(None, AXES, None)),
        check_vma=False,
    )
```

```python
import math

import jax
import jax.numpy as jnp
import numpy as np
from jax import lax
from jax.experimental import pallas as pl
from jax.experimental.pallas import tpu as pltpu
from jax.sharding import PartitionSpec as P

DIR = 36
FREQ = 32
NSUB = 4
NCLASS = 8
LON = 256
K = DIR * FREQ
HALF = K // 2
QUAD = K // 4
ROWS = 10
HALO = NSUB
TAIL = 16
AXES = ("pts", "grp")
VMEM = 28 * 1024 * 1024
OPENING_VMEM = 57 * 1024 * 1024
NEXT_VMEM = 54 * 1024 * 1024

ANGLES = 2.0 * math.pi * (np.arange(DIR) + 0.5) / DIR


def params(limit=VMEM):
    return pltpu.CompilerParams(vmem_limit_bytes=limit)


def held_whole():
    return pl.BlockSpec(memory_space=pltpu.VMEM)


def smem():
    return pl.BlockSpec(memory_space=pltpu.SMEM)


def cost(flops, read):
    return pl.CostEstimate(flops=int(flops), bytes_accessed=int(read), transcendentals=0)


def three_pieces(x):
    hi = x.astype(jnp.bfloat16).astype(jnp.float32)
    mid = (x - hi).astype(jnp.bfloat16).astype(jnp.float32)
    return hi, mid, x - hi - mid


def stack_pieces(pieces):
    which = lax.broadcasted_iota(jnp.int32, (8, LON), 0)
    rows = jnp.zeros((8, LON), jnp.float32)
    for at, piece in enumerate(pieces):
        rows = jnp.where(which == at, jnp.broadcast_to(piece, (8, LON)), rows)
    return jnp.concatenate([rows, jnp.zeros((8, LON), jnp.float32)], axis=0).astype(jnp.bfloat16)


def contract(matrix, spectrum):
    return lax.dot_general(matrix, spectrum, (((0,), (0,)), ((), ())), preferred_element_type=jnp.float32)


def column(vector):
    return jnp.broadcast_to(vector[None, :], (128, K)).T


def point_fields(land_ref, depth_ref, outlets_ref, scale_ref, sea, count, rate):
    sea[...] = land_ref[...].astype(jnp.float32)
    depth = depth_ref[...]
    total = jnp.zeros((ROWS, LON), jnp.float32)
    for c in range(NCLASS):
        total = jnp.where(depth == c, scale_ref[c], total)
    rate[...] = total
    shape = (ROWS, LON)
    flat = lax.broadcasted_iota(jnp.int32, shape, 0) * LON + lax.broadcasted_iota(jnp.int32, shape, 1)
    flat = flat + lax.axis_index(AXES) * (ROWS * LON)
    hits = jnp.zeros(shape, jnp.float32)
    for n in range(outlets_ref.shape[0]):
        hits = hits + jnp.where(flat == outlets_ref[n], 1.0, 0.0)
    count[...] = hits


def first_kernel(pair, opening, x_ref, land_ref, depth_ref, damp_ref, clear_ref, outlets_ref, scale_ref, *rest):
    tables = 4 if opening else 3
    if pair < 2:
        far = [x_ref.at[2 * pair : 2 * pair + 2], rest[tables], land_ref, depth_ref, damp_ref, clear_ref, outlets_ref,
               scale_ref, *rest[:tables]]
        near, sems = rest[-len(far) - 1 : -1], rest[-1]
        rest = rest[: -len(far) - 1]
        copies = [pltpu.make_async_copy(a, b, sems.at[i]) for i, (a, b) in enumerate(zip(far, near))]
        x_ref, jac_ref, land_ref, depth_ref, damp_ref, clear_ref, outlets_ref, scale_ref = near[:8]
        rest = near[8:] + (jac_ref,) + rest[tables + 1 :]
    else:
        near, sems = rest[-2], rest[-1]
        rest = rest[:-2]
        copies = [pltpu.make_async_copy(x_ref.at[2 * pair : 2 * pair + 2], near, sems.at[0])]
        x_ref = near
    for copy in copies:
        copy.start()
    for copy in copies[2:]:
        copy.wait()
    sea, count, rate, held = rest[-4:]
    rest = rest[:-4]
    if opening:
        weight_ref, freq_ref, growth_ref, compass_ref, _, fw_ref, fd_ref, wave_ref = rest[:8]
        fw_ref[...] = column(weight_ref[...])
        fd_ref[...] = column(freq_ref[...])
        hi, mid, low = three_pieces(column(growth_ref[...]) * compass_ref[...])
        lane = lax.broadcasted_iota(jnp.int32, (K, 128), 1)
        wave_ref[...] = jnp.where(lane < 8, hi, jnp.where(lane < 16, mid, low)).astype(jnp.bfloat16)
        outs = rest[8:]
    else:
        fw_ref, fd_ref, wave_ref, jac_ref = rest[:4]
        outs = rest[4:]
    halves, wind_ref = outs[:2], outs[2]
    point_fields(land_ref, depth_ref, outlets_ref, scale_ref, sea, count, rate)
    for copy in copies[:2]:
        copy.wait()

    fw = fw_ref[...]
    fw = jnp.concatenate([fw, fw], axis=1)
    seeds = []
    fields = []
    for e in range(2):
        r = slice(2 * pair + e, 2 * pair + e + 1)
        lone = sea[r, :] * (x_ref[e].astype(jnp.float32) + fw * count[r, :])
        seeds.append(lone.astype(jnp.bfloat16))
        fields.append((rate[r, :], damp_ref[r, :]))
    spectrum = jnp.concatenate(seeds, axis=1)
    for m in range(3):
        rows = slice(m * 384, (m + 1) * 384)
        mixed = contract(jac_ref[:, rows], spectrum)
        fd = fd_ref[rows, :]
        for piece in range(4):
            e, side = divmod(piece, 2)
            lanes = slice(side * 128, (side + 1) * 128)
            at = slice(piece * 128, (piece + 1) * 128)
            v = seeds[e][rows, lanes].astype(jnp.float32)
            held[piece, rows, :] = (
                v + fields[e][0][:, lanes] * mixed[:, at] - (fields[e][1][:, lanes] * fd) * v
            )
    wind = contract(wave_ref[...], spectrum)
    wind = wind[0:8] + wind[8:16] + wind[16:24]
    for e in range(2):
        wind_ref[e] = wind[:, e * LON : (e + 1) * LON]
    for half in range(2):
        for d in range(18):
            for piece in range(4):
                e, side = divmod(piece, 2)
                halves[half][e, d * FREQ : (d + 1) * FREQ, side * 128 : (side + 1) * 128] = held[
                    piece, pl.ds(half * 18 + d, FREQ, stride=DIR), :
                ].astype(jnp.bfloat16)
    if pair != 2:
        for e in range(2):
            r = slice(2 * pair + e, 2 * pair + e + 1)
            pieces = three_pieces(sea[r, :] * clear_ref[r, :])
            halves[0 if pair < 2 else 1][e, HALF : HALF + TAIL, :] = stack_pieces(pieces)


def first_source(pair, opening, x, land, depth, damping, clear, outlets, scale, comps, jacobian):
    sizes = (HALF + TAIL if pair < 2 else HALF, HALF + TAIL if pair > 2 else HALF)
    out_shape = [jax.ShapeDtypeStruct((2, size, LON), jnp.bfloat16) for size in sizes]
    out_shape.append(jax.ShapeDtypeStruct((2, 8, LON), jnp.float32))
    if opening:
        tables = [jax.ShapeDtypeStruct((K, 128), dtype) for dtype in (jnp.float32, jnp.float32, jnp.bfloat16)]
        out_shape = tables + out_shape
    scratch = [pltpu.VMEM((ROWS, LON), jnp.float32)] * 3 + [pltpu.VMEM((4, K, 128), jnp.float32)]
    scratch.append(pltpu.VMEM((2, K, LON), jnp.bfloat16))
    if pair < 2:
        scratch.append(pltpu.VMEM((K, K), jnp.bfloat16))
        scratch += [pltpu.VMEM(a.shape, a.dtype) for a in (land, depth, damping, clear)]
        scratch += [pltpu.SMEM(a.shape, a.dtype) for a in (outlets, scale)]
        scratch += [pltpu.VMEM(a.shape, a.dtype) for a in comps]
    scratch.append(pltpu.SemaphoreType.DMA((12,)))
    anywhere = pl.BlockSpec(memory_space=pl.ANY)
    place = anywhere if pair < 2 else held_whole()

    def body(*refs):
        first_kernel(pair, opening, *refs)

    return pl.pallas_call(
        body,
        grid=(1,),
        in_specs=[anywhere] + [place] * 4 + [place if pair < 2 else smem()] * 2 + [place] * (len(comps) + 1),
        out_specs=[held_whole()] * len(out_shape),
        out_shape=out_shape,
        scratch_shapes=scratch,
        compiler_params=params((OPENING_VMEM, NEXT_VMEM, VMEM, VMEM, VMEM)[pair]),
        cost_estimate=cost(2 * K * K * LON * 2, 4 * K * LON * 2),
        name=f"first_source_{pair}",
    )(x, land, depth, damping, clear, outlets, scale, *comps, jacobian)


def sweep_rows(north, table_ref, courant_ref, pass_rows, emit):
    halves = (slice(0, 128), slice(128, 256))
    lane = lax.broadcasted_iota(jnp.int32, (16, 128), 1)
    for quad in (0, 1) if north else (2, 3):
        east = quad in (0, 3)
        last = lane == 127 if east else lane == 0
        shift = 127 if east else 1
        order = halves if east else halves[::-1]

        def chunk(i, carry, quad=quad, last=last, shift=shift, order=order):
            d = quad * (QUAD // FREQ) + i // 2
            rows = pl.ds(pl.multiple_of((quad % 2) * QUAD + i * 16, 16), 16)
            speed = courant_ref[pl.ds(pl.multiple_of((i % 2) * 16, 16), 16), :]
            across = speed * table_ref[0, d]
            upward = speed * table_ref[1, d]
            centre = 1.0 - across - upward
            upward = upward / centre
            across = across / centre
            walled = jnp.where(last, 0.0, across)
            square = centre * centre

            def advance(v, first):
                turned = [
                    [pltpu.roll(value.astype(jnp.bfloat16), shift, 1).astype(jnp.float32) for value in half[:-1]]
                    for half in v
                ]
                fresh = [[], []]
                for t in range(len(v[0]) - 1):
                    beside = (jnp.where(last, turned[1][t], turned[0][t]), turned[1][t])
                    for half, weight in ((0, across), (1, walled)):
                        fresh[half].append(
                            pass_rows[first + t, :, order[half]]
                            * (v[half][t] + weight * beside[half] + upward * v[half][t + 1])
                        )
                return fresh

            emit(rows, order, advance, square * square)
            return carry

        lax.fori_loop(0, QUAD // 16, chunk, 0, unroll=3)


def own_passage(land_ref, clear_ref, pass_rows, north):
    passage = land_ref[...].astype(jnp.float32) * clear_ref[...]
    for t in range(ROWS):
        own = t if north else ROWS - 1 - t
        pass_rows[t] = jnp.broadcast_to(passage[own : own + 1, :], (16, LON))


def row_of(sources, r, *rest):
    for source in sources:
        if r < source.shape[0]:
            return source[(r, *rest)].astype(jnp.float32)
        r -= source.shape[0]


def inner_kernel(north, table_ref, land_ref, clear_ref, courant_ref, *rest):
    sources, (done, state, pass_rows) = rest[:-3], rest[-3:]
    own_passage(land_ref, clear_ref, pass_rows, north)

    def emit(rows, order, advance, scale):
        v = [[row_of(sources, t if north else ROWS - 1 - t, rows, lanes) for t in range(ROWS)] for lanes in order]
        for s in range(NSUB):
            v = advance(v, 0)
            if s < NSUB - 1:
                for half in range(2):
                    state[s, rows, order[half]] = v[half][-1]
        for half in range(2):
            for t in range(ROWS - NSUB):
                done[t if north else ROWS - NSUB - 1 - t, rows, order[half]] = (scale * v[half][t]).astype(jnp.bfloat16)

    sweep_rows(north, table_ref, courant_ref, pass_rows, emit)


def inner_sweep(north, table, land, clear, courant, sources):
    def body(*refs):
        inner_kernel(north, *refs)

    return pl.pallas_call(
        body,
        in_specs=[smem()] + [held_whole()] * (3 + len(sources)),
        out_specs=[held_whole()] * 2,
        out_shape=[
            jax.ShapeDtypeStruct((6, HALF, LON), jnp.bfloat16),
            jax.ShapeDtypeStruct((3, HALF, LON), jnp.float32),
        ],
        scratch_shapes=[pltpu.VMEM((ROWS, 16, LON), jnp.float32)],
        compiler_params=params(),
        cost_estimate=cost(30 * 7 * K * LON * 40, 60 * K * LON),
        name="inner_sweep_north" if north else "inner_sweep_south",
    )(table, land, clear, courant, *sources)


def outer_kernel(north, begin, count, messages, table_ref, land_ref, clear_ref, courant_ref, first, state, *rest):
    halo, done, pass_rows = rest[:messages], rest[messages], rest[-1]
    state_out = rest[messages + 1] if begin + count < HALO else None

    def halo_row(t, rows, lanes=slice(None)):
        return halo[t // 2][t % 2 if north else 1 - t % 2, rows, lanes].astype(jnp.float32)

    own_passage(land_ref, clear_ref, pass_rows, north)
    for t in range(begin + count):
        pieces = halo_row(t, slice(HALF, HALF + TAIL))
        pass_rows[ROWS + t] = jnp.broadcast_to(pieces[0:1] + pieces[1:2] + pieces[2:3], (16, LON))

    def emit(rows, order, advance, scale):
        v = []
        for lanes in order:
            if begin == 0:
                before = first[1 if north else 0, rows, lanes].astype(jnp.float32)
            else:
                before = halo_row(begin - 1, rows, lanes)
            v.append([before] + [halo_row(begin + t, rows, lanes) for t in range(count)])
        for s in range(NSUB):
            v = advance(v, ROWS - 1 + begin - s)
            if s < NSUB - 1:
                if state_out is not None:
                    for half in range(2):
                        state_out[s, rows, order[half]] = v[half][-1]
                v = [[state[s, rows, lanes]] + half for lanes, half in zip(order, v)]
        for half in range(2):
            for t in range(count):
                done[t if north else count - 1 - t, rows, order[half]] = (scale * v[half][t]).astype(jnp.bfloat16)

    sweep_rows(north, table_ref, courant_ref, pass_rows, emit)


def outer_sweep(north, begin, count, table, land, clear, courant, first, state, halos):
    def body(*refs):
        outer_kernel(north, begin, count, len(halos), *refs)

    out_shape = [jax.ShapeDtypeStruct((count, HALF, LON), jnp.bfloat16)]
    if begin + count < HALO:
        out_shape.append(jax.ShapeDtypeStruct((3, HALF, LON), jnp.float32))
    return pl.pallas_call(
        body,
        in_specs=[smem()] + [held_whole()] * (5 + len(halos)),
        out_specs=[held_whole()] * len(out_shape),
        out_shape=out_shape,
        scratch_shapes=[pltpu.VMEM((ROWS + HALO, 16, LON), jnp.float32)],
        compiler_params=params(),
        cost_estimate=cost(count * 4 * 7 * K * LON * 40, 50 * K * LON),
        name=f"outer_sweep_{'north' if north else 'south'}_{begin}",
    )(table, land, clear, courant, first, state, *halos)


def second_kernel(pair, at_n, at_s, n_ref, s_ref, *refs):
    depth_ref, damp_ref, scale_ref, fd_ref, jac_ref, wave_ref, wind_in = refs[:7]
    out_ref, wind_ref, held = refs[-3:]
    here = slice(2 * pair, 2 * pair + 2)
    depth = depth_ref[here, :]
    rate = jnp.zeros((2, LON), jnp.float32)
    for c in range(NCLASS):
        rate = jnp.where(depth == c, scale_ref[c], rate)
    damp = damp_ref[here, :]
    for half, ref, at in ((0, n_ref, at_n), (1, s_ref, at_s)):
        for d in range(18):
            for piece in range(4):
                e, side = divmod(piece, 2)
                held[piece, pl.ds(half * 18 + d, FREQ, stride=DIR), :] = ref[
                    at + e, d * FREQ : (d + 1) * FREQ, side * 128 : (side + 1) * 128
                ].astype(jnp.float32)
    spectrum = jnp.concatenate([held[piece].astype(jnp.bfloat16) for piece in range(4)], axis=1)
    for m in range(3):
        rows = slice(m * 384, (m + 1) * 384)
        mixed = contract(jac_ref[:, rows], spectrum)
        fd = fd_ref[rows, :]
        for piece in range(4):
            e, side = divmod(piece, 2)
            lanes = slice(side * 128, (side + 1) * 128)
            at = slice(piece * 128, (piece + 1) * 128)
            v = held[piece, rows, :]
            out_ref[e, rows, lanes] = (
                v + rate[e : e + 1, lanes] * mixed[:, at] - (damp[e : e + 1, lanes] * fd) * v
            ).astype(jnp.bfloat16)
    wind = contract(wave_ref[...], spectrum)
    wind = wind[0:8] + wind[8:16] + wind[16:24]
    for e in range(2):
        wind_ref[e] = (wind_in[e] + wind[:, e * LON : (e + 1) * LON])[:2]


def second_source(pair, north, at_n, south, at_s, before, depth, damping, scale, fd, jac, wave, wind):
    def body(*refs):
        second_kernel(pair, at_n, at_s, *refs)

    return pl.pallas_call(
        body,
        grid=(1,),
        in_specs=[held_whole()] * 4
        + [smem()]
        + [held_whole()] * 4
        + [pl.BlockSpec(memory_space=pl.ANY)] * len(before),
        out_specs=[pl.BlockSpec((2, K, LON), lambda i: (pair, 0, 0)), pl.BlockSpec((2, 2, LON), lambda i: (pair, 0, 0))],
        out_shape=[
            jax.ShapeDtypeStruct((ROWS, K, LON), jnp.bfloat16),
            jax.ShapeDtypeStruct((ROWS, 2, LON), jnp.float32),
        ],
        input_output_aliases={9: 0, 10: 1} if before else {},
        scratch_shapes=[pltpu.VMEM((4, K, 128), jnp.float32)],
        compiler_params=params(),
        cost_estimate=cost(2 * K * K * LON * 2, 4 * K * LON * 2),
        name=f"second_source_{pair}",
    )(north, south, depth, damping, scale, fd, jac, wave, wind, *before)


def body(
    adjoint_in,
    land_sea,
    depth_class,
    damping,
    transparency,
    outlets,
    flux_weight,
    jacobian,
    source_scale,
    freq_damp,
    courant,
    wind_growth,
):
    devices = lax.axis_size(AXES)
    x = adjoint_in.transpose(1, 0, 2)
    compass = np.zeros((K, 128), np.float32)
    for at in range(3):
        compass[:, 8 * at] = np.tile(np.cos(ANGLES), FREQ)
        compass[:, 8 * at + 1] = np.tile(np.sin(ANGLES), FREQ)
    comps = (flux_weight, freq_damp, wind_growth, jnp.asarray(compass))
    common = (x, land_sea, depth_class, damping, transparency, outlets, source_scale)
    down = [(i + 1, i) for i in range(devices - 1)]
    up = [(i, i + 1) for i in range(devices - 1)]
    speed = jnp.broadcast_to(courant[:, None], (FREQ, 128))
    table = jnp.asarray(np.abs(np.stack([np.cos(ANGLES), np.sin(ANGLES)])), jnp.float32)
    local = (table, land_sea, transparency, speed)
    n, s, winds, halo_n, halo_s = {}, {}, {}, {}, {}

    fw, fd, wave, n[0], s[0], winds[0] = first_source(0, True, *common, comps, jacobian)
    halo_n[0] = lax.ppermute(n[0], AXES, down)
    comps = (fw, fd, wave)
    for pair in (1, 4, 3, 2):
        n[pair], s[pair], winds[pair] = first_source(pair, False, *common, comps, jacobian)
    halo_n[1] = lax.ppermute(n[1], AXES, down)
    in_n, state_n = inner_sweep(True, *local, [n[pair] for pair in range(5)])
    in_s, state_s = inner_sweep(False, *local, [s[pair] for pair in range(5)])
    s[4], state_s = lax.optimization_barrier((s[4], state_s))
    halo_s[0] = lax.ppermute(s[4], AXES, up)
    last = (depth_class, damping, source_scale, fd, jacobian, wave)
    part = second_source(2, in_n, 4, in_s, 0, (), *last, winds[2])
    (edge,) = outer_sweep(True, 0, HALO, *local, n[4], state_n, (halo_n[0], halo_n[1]))
    s[3], edge = lax.optimization_barrier((s[3], edge))
    halo_s[1] = lax.ppermute(s[3], AXES, up)
    part = second_source(3, edge, 0, in_s, 2, part, *last, winds[3])
    part = second_source(4, edge, 2, in_s, 4, part, *last, winds[4])
    state_s, *part = lax.optimization_barrier((state_s, *part))
    edge, state_s = outer_sweep(False, 0, 2, *local, s[0], state_s, (halo_s[0],))
    part = second_source(1, in_n, 2, edge, 0, part, *last, winds[1])
    state_s, *part = lax.optimization_barrier((state_s, *part))
    (edge,) = outer_sweep(False, 2, 2, *local, s[0], state_s, (halo_s[0], halo_s[1]))
    out, wind_out = second_source(0, in_n, 0, edge, 0, part, *last, winds[0])
    return out.transpose(1, 0, 2), wind_out.transpose(1, 0, 2)


def solution(mesh):
    rows = P(AXES, None)
    placed = (P(None, AXES, None), rows, rows, rows, rows, P(), P(), P(), P(), P(), P(), P())
    return jax.shard_map(
        body,
        mesh=mesh,
        in_specs=placed,
        out_specs=(P(None, AXES, None), P(None, AXES, None)),
        check_vma=False,
    )
```

```python
import math

import jax
import jax.numpy as jnp
import numpy as np
from jax import lax
from jax.experimental import pallas as pl
from jax.experimental.pallas import tpu as pltpu
from jax.sharding import PartitionSpec as P

DIR = 36
FREQ = 32
NSUB = 4
NCLASS = 8
LON = 256
K = DIR * FREQ
HALF = K // 2
QUAD = K // 4
ROWS = 10
HALO = NSUB
TAIL = 16
AXES = ("pts", "grp")
VMEM = 28 * 1024 * 1024
FIRST_VMEM = {0: 57 * 1024 * 1024, 1: 54 * 1024 * 1024, 4: 28 * 1024 * 1024}

ANGLES = 2.0 * math.pi * (np.arange(DIR) + 0.5) / DIR


def params(limit=VMEM):
    return pltpu.CompilerParams(vmem_limit_bytes=limit)


def held_whole():
    return pl.BlockSpec(memory_space=pltpu.VMEM)


def smem():
    return pl.BlockSpec(memory_space=pltpu.SMEM)


def cost(flops, read):
    return pl.CostEstimate(flops=int(flops), bytes_accessed=int(read), transcendentals=0)


def three_pieces(x):
    hi = x.astype(jnp.bfloat16).astype(jnp.float32)
    mid = (x - hi).astype(jnp.bfloat16).astype(jnp.float32)
    return hi, mid, x - hi - mid


def stack_pieces(pieces):
    which = lax.broadcasted_iota(jnp.int32, (8, LON), 0)
    rows = jnp.zeros((8, LON), jnp.float32)
    for at, piece in enumerate(pieces):
        rows = jnp.where(which == at, jnp.broadcast_to(piece, (8, LON)), rows)
    return jnp.concatenate([rows, jnp.zeros((8, LON), jnp.float32)], axis=0).astype(jnp.bfloat16)


def contract(matrix, spectrum):
    return lax.dot_general(matrix, spectrum, (((0,), (0,)), ((), ())), preferred_element_type=jnp.float32)


def column(vector):
    return jnp.broadcast_to(vector[None, :], (128, K)).T


def point_fields(land_ref, depth_ref, outlets_ref, scale_ref, sea, count, rate):
    sea[...] = land_ref[...].astype(jnp.float32)
    depth = depth_ref[...]
    total = jnp.zeros((ROWS, LON), jnp.float32)
    for c in range(NCLASS):
        total = jnp.where(depth == c, scale_ref[c], total)
    rate[...] = total
    shape = (ROWS, LON)
    flat = lax.broadcasted_iota(jnp.int32, shape, 0) * LON + lax.broadcasted_iota(jnp.int32, shape, 1)
    flat = flat + lax.axis_index(AXES) * (ROWS * LON)
    hits = jnp.zeros(shape, jnp.float32)
    for n in range(outlets_ref.shape[0]):
        hits = hits + jnp.where(flat == outlets_ref[n], 1.0, 0.0)
    count[...] = hits


def first_kernel(pairs, x_ref, jac_hbm, *refs):
    opening = pairs[0] == 0
    tables = 4 if opening else 3
    far = refs[: 6 + tables]
    outs = refs[6 + tables : -7 - len(far)]
    sea, count, rate, held, x_near, jac_ref = refs[-7 - len(far) : -1 - len(far)]
    near, sems = refs[-1 - len(far) : -1], refs[-1]
    copies = [pltpu.make_async_copy(a, b, sems.at[i]) for i, (a, b) in enumerate(zip(far, near))]
    waits = [pltpu.make_async_copy(jac_hbm, jac_ref, sems.at[len(far)])]
    for i, pair in enumerate(pairs):
        waits.append(
            pltpu.make_async_copy(
                x_ref.at[2 * pair : 2 * pair + 2], x_near.at[2 * i : 2 * i + 2], sems.at[len(far) + 1 + i]
            )
        )
    for copy in copies + waits:
        copy.start()
    for copy in copies:
        copy.wait()
    land_ref, depth_ref, damp_ref, clear_ref, outlets_ref, scale_ref = near[:6]
    if opening:
        weight_ref, freq_ref, growth_ref, compass_ref = near[6:]
        fw_ref, fd_ref, wave_ref = outs[:3]
        outs = outs[3:]
        fw_ref[...] = column(weight_ref[...])
        fd_ref[...] = column(freq_ref[...])
        hi, mid, low = three_pieces(column(growth_ref[...]) * compass_ref[...])
        lane = lax.broadcasted_iota(jnp.int32, (K, 128), 1)
        wave_ref[...] = jnp.where(lane < 8, hi, jnp.where(lane < 16, mid, low)).astype(jnp.bfloat16)
    else:
        fw_ref, fd_ref, wave_ref = near[6:]
    point_fields(land_ref, depth_ref, outlets_ref, scale_ref, sea, count, rate)
    waits[0].wait()

    for i, pair in enumerate(pairs):
        waits[1 + i].wait()
        to = 2 * i if opening else 0
        halves, wind_ref = (outs[:2], outs[2]) if opening else (outs[3 * i : 3 * i + 2], outs[3 * i + 2])
        fw = fw_ref[...]
        fw = jnp.concatenate([fw, fw], axis=1)
        seeds = []
        fields = []
        for e in range(2):
            r = slice(2 * pair + e, 2 * pair + e + 1)
            lone = sea[r, :] * (x_near[2 * i + e].astype(jnp.float32) + fw * count[r, :])
            seeds.append(lone.astype(jnp.bfloat16))
            fields.append((rate[r, :], damp_ref[r, :]))
        spectrum = jnp.concatenate(seeds, axis=1)
        for m in range(3):
            rows = slice(m * 384, (m + 1) * 384)
            mixed = contract(jac_ref[:, rows], spectrum)
            fd = fd_ref[rows, :]
            for piece in range(4):
                e, side = divmod(piece, 2)
                lanes = slice(side * 128, (side + 1) * 128)
                at = slice(piece * 128, (piece + 1) * 128)
                v = seeds[e][rows, lanes].astype(jnp.float32)
                held[piece, rows, :] = (
                    v + fields[e][0][:, lanes] * mixed[:, at] - (fields[e][1][:, lanes] * fd) * v
                )
        wind = contract(wave_ref[...], spectrum)
        wind = wind[0:8] + wind[8:16] + wind[16:24]
        for e in range(2):
            wind_ref[to + e] = wind[:, e * LON : (e + 1) * LON]
        for half in range(2):
            for d in range(18):
                for piece in range(4):
                    e, side = divmod(piece, 2)
                    halves[half][to + e, d * FREQ : (d + 1) * FREQ, side * 128 : (side + 1) * 128] = held[
                        piece, pl.ds(half * 18 + d, FREQ, stride=DIR), :
                    ].astype(jnp.bfloat16)
        if pair != 2:
            for e in range(2):
                r = slice(2 * pair + e, 2 * pair + e + 1)
                pieces = three_pieces(sea[r, :] * clear_ref[r, :])
                halves[0 if pair < 2 else 1][to + e, HALF : HALF + TAIL, :] = stack_pieces(pieces)


def first_source(pairs, x, jacobian, land, depth, damping, clear, outlets, scale, comps):
    out_shape = []
    if pairs[0] == 0:
        out_shape += [jax.ShapeDtypeStruct((K, 128), dtype) for dtype in (jnp.float32, jnp.float32, jnp.bfloat16)]
    for pair in pairs[:1] if pairs[0] == 0 else pairs:
        count_rows = 2 * len(pairs) if pairs[0] == 0 else 2
        for size in (HALF + TAIL if pair < 2 else HALF, HALF + TAIL if pair > 2 else HALF):
            out_shape.append(jax.ShapeDtypeStruct((count_rows, size, LON), jnp.bfloat16))
        out_shape.append(jax.ShapeDtypeStruct((count_rows, 8, LON), jnp.float32))
    small = (land, depth, damping, clear, outlets, scale, *comps)
    scratch = [pltpu.VMEM((ROWS, LON), jnp.float32)] * 3 + [pltpu.VMEM((4, K, 128), jnp.float32)]
    scratch += [pltpu.VMEM((2 * len(pairs), K, LON), jnp.bfloat16), pltpu.VMEM((K, K), jnp.bfloat16)]
    for at, a in enumerate(small):
        scratch.append((pltpu.SMEM if at in (4, 5) else pltpu.VMEM)(a.shape, a.dtype))
    scratch.append(pltpu.SemaphoreType.DMA((len(small) + 1 + len(pairs),)))

    def body(*refs):
        first_kernel(pairs, *refs)

    return pl.pallas_call(
        body,
        in_specs=[pl.BlockSpec(memory_space=pl.ANY)] * (2 + len(small)),
        out_specs=[held_whole()] * len(out_shape),
        out_shape=out_shape,
        scratch_shapes=scratch,
        compiler_params=params(FIRST_VMEM[pairs[0]]),
        cost_estimate=cost(2 * K * K * LON * 2 * len(pairs), 4 * K * LON * 2 * len(pairs)),
        name=f"first_source_{pairs[0]}",
    )(x, jacobian, *small)


def sweep_rows(north, table_ref, courant_ref, pass_rows, emit):
    halves = (slice(0, 128), slice(128, 256))
    lane = lax.broadcasted_iota(jnp.int32, (16, 128), 1)
    for quad in (0, 1) if north else (2, 3):
        east = quad in (0, 3)
        last = lane == 127 if east else lane == 0
        shift = 127 if east else 1
        order = halves if east else halves[::-1]

        def chunk(i, carry, quad=quad, last=last, shift=shift, order=order):
            d = quad * (QUAD // FREQ) + i // 2
            rows = pl.ds(pl.multiple_of((quad % 2) * QUAD + i * 16, 16), 16)
            speed = courant_ref[pl.ds(pl.multiple_of((i % 2) * 16, 16), 16), :]
            across = speed * table_ref[0, d]
            upward = speed * table_ref[1, d]
            centre = 1.0 - across - upward
            upward = upward / centre
            across = across / centre
            walled = jnp.where(last, 0.0, across)
            square = centre * centre

            def advance(v, first):
                turned = [
                    [pltpu.roll(value.astype(jnp.bfloat16), shift, 1).astype(jnp.float32) for value in half[:-1]]
                    for half in v
                ]
                fresh = [[], []]
                for t in range(len(v[0]) - 1):
                    beside = (jnp.where(last, turned[1][t], turned[0][t]), turned[1][t])
                    for half, weight in ((0, across), (1, walled)):
                        fresh[half].append(
                            pass_rows[first + t, :, order[half]]
                            * (v[half][t] + weight * beside[half] + upward * v[half][t + 1])
                        )
                return fresh

            emit(rows, order, advance, square * square)
            return carry

        lax.fori_loop(0, QUAD // 16, chunk, 0, unroll=3)


def own_passage(land_ref, clear_ref, pass_rows, north):
    passage = land_ref[...].astype(jnp.float32) * clear_ref[...]
    for t in range(ROWS):
        own = t if north else ROWS - 1 - t
        pass_rows[t] = jnp.broadcast_to(passage[own : own + 1, :], (16, LON))


def row_of(sources, r, *rest):
    for source in sources:
        if r < source.shape[0]:
            return source[(r, *rest)].astype(jnp.float32)
        r -= source.shape[0]


def inner_kernel(north, table_ref, land_ref, clear_ref, courant_ref, *rest):
    sources, (done, state, pass_rows) = rest[:-3], rest[-3:]
    own_passage(land_ref, clear_ref, pass_rows, north)

    def emit(rows, order, advance, scale):
        v = [[row_of(sources, t if north else ROWS - 1 - t, rows, lanes) for t in range(ROWS)] for lanes in order]
        for s in range(NSUB):
            v = advance(v, 0)
            if s < NSUB - 1:
                for half in range(2):
                    state[s, rows, order[half]] = v[half][-1]
        for half in range(2):
            for t in range(ROWS - NSUB):
                done[t if north else ROWS - NSUB - 1 - t, rows, order[half]] = (scale * v[half][t]).astype(jnp.bfloat16)

    sweep_rows(north, table_ref, courant_ref, pass_rows, emit)


def inner_sweep(north, table, land, clear, courant, sources):
    def body(*refs):
        inner_kernel(north, *refs)

    return pl.pallas_call(
        body,
        in_specs=[smem()] + [held_whole()] * (3 + len(sources)),
        out_specs=[held_whole()] * 2,
        out_shape=[
            jax.ShapeDtypeStruct((6, HALF, LON), jnp.bfloat16),
            jax.ShapeDtypeStruct((3, HALF, LON), jnp.float32),
        ],
        scratch_shapes=[pltpu.VMEM((ROWS, 16, LON), jnp.float32)],
        compiler_params=params(),
        cost_estimate=cost(30 * 7 * K * LON * 40, 60 * K * LON),
        name="inner_sweep_north" if north else "inner_sweep_south",
    )(table, land, clear, courant, *sources)


def outer_kernel(north, begin, count, messages, table_ref, land_ref, clear_ref, courant_ref, first, state, *rest):
    halo, done, pass_rows = rest[:messages], rest[messages], rest[-1]
    state_out = rest[messages + 1] if begin + count < HALO else None

    def halo_row(t, rows, lanes=slice(None)):
        place = (t // 2, t % 2 if north else 1 - t % 2)
        return halo[place[0]][place[1], rows, lanes].astype(jnp.float32)

    own_passage(land_ref, clear_ref, pass_rows, north)
    for t in range(begin + count):
        pieces = halo_row(t, slice(HALF, HALF + TAIL))
        pass_rows[ROWS + t] = jnp.broadcast_to(pieces[0:1] + pieces[1:2] + pieces[2:3], (16, LON))

    def emit(rows, order, advance, scale):
        v = []
        for lanes in order:
            if begin == 0:
                before = first[1 if north else 0, rows, lanes].astype(jnp.float32)
            else:
                before = halo_row(begin - 1, rows, lanes)
            v.append([before] + [halo_row(begin + t, rows, lanes) for t in range(count)])
        for s in range(NSUB):
            v = advance(v, ROWS - 1 + begin - s)
            if s < NSUB - 1:
                if state_out is not None:
                    for half in range(2):
                        state_out[s, rows, order[half]] = v[half][-1]
                v = [[state[s, rows, lanes]] + half for lanes, half in zip(order, v)]
        for half in range(2):
            for t in range(count):
                done[t if north else count - 1 - t, rows, order[half]] = (scale * v[half][t]).astype(jnp.bfloat16)

    sweep_rows(north, table_ref, courant_ref, pass_rows, emit)


def outer_sweep(north, begin, count, table, land, clear, courant, first, state, halos):
    def body(*refs):
        outer_kernel(north, begin, count, len(halos), *refs)

    out_shape = [jax.ShapeDtypeStruct((count, HALF, LON), jnp.bfloat16)]
    if begin + count < HALO:
        out_shape.append(jax.ShapeDtypeStruct((3, HALF, LON), jnp.float32))
    return pl.pallas_call(
        body,
        in_specs=[smem()] + [held_whole()] * (5 + len(halos)),
        out_specs=[held_whole()] * len(out_shape),
        out_shape=out_shape,
        scratch_shapes=[pltpu.VMEM((ROWS + HALO, 16, LON), jnp.float32)],
        compiler_params=params(),
        cost_estimate=cost(count * 4 * 7 * K * LON * 40, 50 * K * LON),
        name=f"outer_sweep_{'north' if north else 'south'}_{begin}",
    )(table, land, clear, courant, first, state, *halos)


def second_kernel(jobs, count, *refs):
    sources, refs = refs[:count], refs[count:]
    depth_ref, damp_ref, scale_ref, fd_ref, jac_ref, wave_ref = refs[:6]
    out_ref, wind_ref, held = refs[-3:]

    def run(pair, south_at, wind_at):
        north_at = (0, 2 * pair) if pair < 3 else (1, 2 * pair - 6)
        here = slice(2 * pair, 2 * pair + 2)
        depth = depth_ref[here, :]
        rate = jnp.zeros((2, LON), jnp.float32)
        for c in range(NCLASS):
            rate = jnp.where(depth == c, scale_ref[c], rate)
        damp = damp_ref[here, :]
        for half, (source, at) in enumerate((north_at, south_at)):
            for d in range(18):
                for piece in range(4):
                    e, side = divmod(piece, 2)
                    held[piece, pl.ds(half * 18 + d, FREQ, stride=DIR), :] = sources[source][
                        at + e, d * FREQ : (d + 1) * FREQ, side * 128 : (side + 1) * 128
                    ].astype(jnp.float32)
        spectrum = jnp.concatenate([held[piece].astype(jnp.bfloat16) for piece in range(4)], axis=1)
        for m in range(3):
            rows = slice(m * 384, (m + 1) * 384)
            mixed = contract(jac_ref[:, rows], spectrum)
            fd = fd_ref[rows, :]
            for piece in range(4):
                e, side = divmod(piece, 2)
                lanes = slice(side * 128, (side + 1) * 128)
                at = slice(piece * 128, (piece + 1) * 128)
                v = held[piece, rows, :]
                out_ref[e, rows, lanes] = (
                    v + rate[e : e + 1, lanes] * mixed[:, at] - (damp[e : e + 1, lanes] * fd) * v
                ).astype(jnp.bfloat16)
        wind = contract(wave_ref[...], spectrum)
        wind = wind[0:8] + wind[8:16] + wind[16:24]
        for e in range(2):
            wind_ref[e] = (sources[wind_at][e] + wind[:, e * LON : (e + 1) * LON])[:2]

    step = pl.program_id(0)
    for i, job in enumerate(jobs):
        pl.when(step == i)(lambda job=job: run(*job))


def second_source(jobs, sources, before, depth, damping, scale, fd, jac, wave):
    start = jobs[0][0]

    def body(*refs):
        second_kernel(jobs, len(sources), *refs)

    return pl.pallas_call(
        body,
        grid=(len(jobs),),
        in_specs=[held_whole()] * (len(sources) + 2)
        + [smem()]
        + [held_whole()] * 3
        + [pl.BlockSpec(memory_space=pl.ANY)] * len(before),
        out_specs=[
            pl.BlockSpec((2, K, LON), lambda i: (i + start, 0, 0)),
            pl.BlockSpec((2, 2, LON), lambda i: (i + start, 0, 0)),
        ],
        out_shape=[
            jax.ShapeDtypeStruct((ROWS, K, LON), jnp.bfloat16),
            jax.ShapeDtypeStruct((ROWS, 2, LON), jnp.float32),
        ],
        input_output_aliases={len(sources) + 6: 0, len(sources) + 7: 1} if before else {},
        scratch_shapes=[pltpu.VMEM((4, K, 128), jnp.float32)],
        compiler_params=params(),
        cost_estimate=cost(2 * K * K * LON * 2 * len(jobs), 4 * K * LON * 2 * len(jobs)),
        name=f"second_source_{start}",
    )(*sources, depth, damping, scale, fd, jac, wave, *before)


def body(
    adjoint_in,
    land_sea,
    depth_class,
    damping,
    transparency,
    outlets,
    flux_weight,
    jacobian,
    source_scale,
    freq_damp,
    courant,
    wind_growth,
):
    devices = lax.axis_size(AXES)
    x = adjoint_in.transpose(1, 0, 2)
    compass = np.zeros((K, 128), np.float32)
    for at in range(3):
        compass[:, 8 * at] = np.tile(np.cos(ANGLES), FREQ)
        compass[:, 8 * at + 1] = np.tile(np.sin(ANGLES), FREQ)
    comps = (flux_weight, freq_damp, wind_growth, jnp.asarray(compass))
    common = (land_sea, depth_class, damping, transparency, outlets, source_scale)
    down = [(i + 1, i) for i in range(devices - 1)]
    up = [(i, i + 1) for i in range(devices - 1)]
    speed = jnp.broadcast_to(courant[:, None], (FREQ, 128))
    table = jnp.asarray(np.abs(np.stack([np.cos(ANGLES), np.sin(ANGLES)])), jnp.float32)
    local = (table, land_sea, transparency, speed)
    n, s, winds, halo_s = {}, {}, {}, {}

    fw, fd, wave, n[0], s[0], winds[0] = first_source((0,), x, jacobian, *common, comps)
    halo_n = [lax.ppermute(n[0], AXES, down)]
    comps = (fw, fd, wave)
    n[1], s[1], winds[1] = first_source((1,), x, jacobian, *common, comps)
    halo_n.append(lax.ppermute(n[1], AXES, down))
    rest = (4, 3, 2)
    parts = first_source(rest, x, jacobian, *common, comps)
    for i, pair in enumerate(rest):
        n[pair], s[pair], winds[pair] = parts[3 * i : 3 * i + 3]
    in_s, state_s = inner_sweep(False, *local, [s[pair] for pair in range(5)])
    s[4], state_s, n[2] = lax.optimization_barrier((s[4], state_s, n[2]))
    halo_s[0] = lax.ppermute(s[4], AXES, up)
    in_n, state_n = inner_sweep(True, *local, [n[pair] for pair in range(5)])
    s[3], state_n = lax.optimization_barrier((s[3], state_n))
    halo_s[1] = lax.ppermute(s[3], AXES, up)
    last = (depth_class, damping, source_scale, fd, jacobian, wave)
    (edge,) = outer_sweep(True, 0, HALO, *local, n[4], state_n, halo_n)
    jobs = ((2, (2, 0), 3), (3, (2, 2), 4), (4, (2, 4), 5))
    part = second_source(jobs, (in_n, edge, in_s, winds[2], winds[3], winds[4]), (), *last)
    state_s, *part = lax.optimization_barrier((state_s, *part))
    edge, state_s = outer_sweep(False, 0, 2, *local, s[0], state_s, (halo_s[0],))
    part = second_source(((1, (1, 0), 2),), (in_n, edge, winds[1]), part, *last)
    state_s, *part = lax.optimization_barrier((state_s, *part))
    (edge,) = outer_sweep(False, 2, 2, *local, s[0], state_s, (halo_s[0], halo_s[1]))
    out, wind_out = second_source(((0, (1, 0), 2),), (in_n, edge, winds[0]), part, *last)
    return out.transpose(1, 0, 2), wind_out.transpose(1, 0, 2)


def solution(mesh):
    rows = P(AXES, None)
    placed = (P(None, AXES, None), rows, rows, rows, rows, P(), P(), P(), P(), P(), P(), P())
    return jax.shard_map(
        body,
        mesh=mesh,
        in_specs=placed,
        out_specs=(P(None, AXES, None), P(None, AXES, None)),
        check_vma=False,
    )
```

```python
import math

import jax
import jax.numpy as jnp
import numpy as np
from jax import lax
from jax.experimental import pallas as pl
from jax.experimental.pallas import tpu as pltpu
from jax.sharding import PartitionSpec as P

DIR = 36
FREQ = 32
NSUB = 4
NCLASS = 8
LON = 256
K = DIR * FREQ
HALF = K // 2
QUAD = K // 4
ROWS = 10
HALO = NSUB
TAIL = 16
AXES = ("pts", "grp")
VMEM = 28 * 1024 * 1024
FIRST_VMEM = {0: 57 * 1024 * 1024, 1: 54 * 1024 * 1024, 4: 28 * 1024 * 1024}

ANGLES = 2.0 * math.pi * (np.arange(DIR) + 0.5) / DIR


def params(limit=VMEM):
    return pltpu.CompilerParams(vmem_limit_bytes=limit)


def held_whole():
    return pl.BlockSpec(memory_space=pltpu.VMEM)


def smem():
    return pl.BlockSpec(memory_space=pltpu.SMEM)


def cost(flops, read):
    return pl.CostEstimate(flops=int(flops), bytes_accessed=int(read), transcendentals=0)


def three_pieces(x):
    hi = x.astype(jnp.bfloat16).astype(jnp.float32)
    mid = (x - hi).astype(jnp.bfloat16).astype(jnp.float32)
    return hi, mid, x - hi - mid


def stack_pieces(pieces):
    which = lax.broadcasted_iota(jnp.int32, (8, LON), 0)
    rows = jnp.zeros((8, LON), jnp.float32)
    for at, piece in enumerate(pieces):
        rows = jnp.where(which == at, jnp.broadcast_to(piece, (8, LON)), rows)
    return jnp.concatenate([rows, jnp.zeros((8, LON), jnp.float32)], axis=0).astype(jnp.bfloat16)


def contract(matrix, spectrum):
    return lax.dot_general(matrix, spectrum, (((0,), (0,)), ((), ())), preferred_element_type=jnp.float32)


def column(vector):
    return jnp.broadcast_to(vector[None, :], (128, K)).T


def point_fields(land_ref, depth_ref, outlets_ref, scale_ref, sea, count, rate):
    sea[...] = land_ref[...].astype(jnp.float32)
    depth = depth_ref[...]
    total = jnp.zeros((ROWS, LON), jnp.float32)
    for c in range(NCLASS):
        total = jnp.where(depth == c, scale_ref[c], total)
    rate[...] = total
    shape = (ROWS, LON)
    flat = lax.broadcasted_iota(jnp.int32, shape, 0) * LON + lax.broadcasted_iota(jnp.int32, shape, 1)
    flat = flat + lax.axis_index(AXES) * (ROWS * LON)
    hits = jnp.zeros(shape, jnp.float32)
    for n in range(outlets_ref.shape[0]):
        hits = hits + jnp.where(flat == outlets_ref[n], 1.0, 0.0)
    count[...] = hits


def first_kernel(pairs, x_ref, jac_hbm, *refs):
    opening = pairs[0] == 0
    tables = 4 if opening else 3
    far = refs[: 6 + tables]
    outs = refs[6 + tables : -7 - len(far)]
    sea, count, rate, held, x_near, jac_ref = refs[-7 - len(far) : -1 - len(far)]
    near, sems = refs[-1 - len(far) : -1], refs[-1]
    copies = [pltpu.make_async_copy(a, b, sems.at[i]) for i, (a, b) in enumerate(zip(far, near))]
    chunks = [slice(m * 384, (m + 1) * 384) for m in range(3)]
    jac_copies = [
        pltpu.make_async_copy(jac_hbm.at[:, rows], jac_ref.at[:, rows], sems.at[len(far) + m])
        for m, rows in enumerate(chunks)
    ]
    x_copies = [
        pltpu.make_async_copy(
            x_ref.at[2 * pair : 2 * pair + 2], x_near.at[2 * i : 2 * i + 2], sems.at[len(far) + 3 + i]
        )
        for i, pair in enumerate(pairs)
    ]
    for copy in copies + x_copies[:1] + jac_copies + x_copies[1:]:
        copy.start()
    for copy in copies:
        copy.wait()
    land_ref, depth_ref, damp_ref, clear_ref, outlets_ref, scale_ref = near[:6]
    if opening:
        weight_ref, freq_ref, growth_ref, compass_ref = near[6:]
        fw_ref, fd_ref, wave_ref = outs[:3]
        outs = outs[3:]
        fw_ref[...] = column(weight_ref[...])
        fd_ref[...] = column(freq_ref[...])
        hi, mid, low = three_pieces(column(growth_ref[...]) * compass_ref[...])
        lane = lax.broadcasted_iota(jnp.int32, (K, 128), 1)
        wave_ref[...] = jnp.where(lane < 8, hi, jnp.where(lane < 16, mid, low)).astype(jnp.bfloat16)
    else:
        fw_ref, fd_ref, wave_ref = near[6:]
    point_fields(land_ref, depth_ref, outlets_ref, scale_ref, sea, count, rate)

    for i, pair in enumerate(pairs):
        x_copies[i].wait()
        to = 2 * i if opening else 0
        halves, wind_ref = (outs[:2], outs[2]) if opening else (outs[3 * i : 3 * i + 2], outs[3 * i + 2])
        fw = fw_ref[...]
        fw = jnp.concatenate([fw, fw], axis=1)
        seeds = []
        fields = []
        for e in range(2):
            r = slice(2 * pair + e, 2 * pair + e + 1)
            lone = sea[r, :] * (x_near[2 * i + e].astype(jnp.float32) + fw * count[r, :])
            seeds.append(lone.astype(jnp.bfloat16))
            fields.append((rate[r, :], damp_ref[r, :]))
        spectrum = jnp.concatenate(seeds, axis=1)
        for m, rows in enumerate(chunks):
            if i == 0:
                jac_copies[m].wait()
            mixed = contract(jac_ref[:, rows], spectrum)
            fd = fd_ref[rows, :]
            for piece in range(4):
                e, side = divmod(piece, 2)
                lanes = slice(side * 128, (side + 1) * 128)
                at = slice(piece * 128, (piece + 1) * 128)
                v = seeds[e][rows, lanes].astype(jnp.float32)
                held[piece, rows, :] = (
                    v + fields[e][0][:, lanes] * mixed[:, at] - (fields[e][1][:, lanes] * fd) * v
                )
        wind = contract(wave_ref[...], spectrum)
        wind = wind[0:8] + wind[8:16] + wind[16:24]
        for e in range(2):
            wind_ref[to + e] = wind[:, e * LON : (e + 1) * LON]
        for half in range(2):
            for d in range(18):
                for piece in range(4):
                    e, side = divmod(piece, 2)
                    halves[half][to + e, d * FREQ : (d + 1) * FREQ, side * 128 : (side + 1) * 128] = held[
                        piece, pl.ds(half * 18 + d, FREQ, stride=DIR), :
                    ].astype(jnp.bfloat16)
        if pair != 2:
            for e in range(2):
                r = slice(2 * pair + e, 2 * pair + e + 1)
                pieces = three_pieces(sea[r, :] * clear_ref[r, :])
                halves[0 if pair < 2 else 1][to + e, HALF : HALF + TAIL, :] = stack_pieces(pieces)


def first_source(pairs, x, jacobian, land, depth, damping, clear, outlets, scale, comps):
    out_shape = []
    if pairs[0] == 0:
        out_shape += [jax.ShapeDtypeStruct((K, 128), dtype) for dtype in (jnp.float32, jnp.float32, jnp.bfloat16)]
    for pair in pairs[:1] if pairs[0] == 0 else pairs:
        count_rows = 2 * len(pairs) if pairs[0] == 0 else 2
        for size in (HALF + TAIL if pair < 2 else HALF, HALF + TAIL if pair > 2 else HALF):
            out_shape.append(jax.ShapeDtypeStruct((count_rows, size, LON), jnp.bfloat16))
        out_shape.append(jax.ShapeDtypeStruct((count_rows, 8, LON), jnp.float32))
    small = (land, depth, damping, clear, outlets, scale, *comps)
    scratch = [pltpu.VMEM((ROWS, LON), jnp.float32)] * 3 + [pltpu.VMEM((4, K, 128), jnp.float32)]
    scratch += [pltpu.VMEM((2 * len(pairs), K, LON), jnp.bfloat16), pltpu.VMEM((K, K), jnp.bfloat16)]
    for at, a in enumerate(small):
        scratch.append((pltpu.SMEM if at in (4, 5) else pltpu.VMEM)(a.shape, a.dtype))
    scratch.append(pltpu.SemaphoreType.DMA((len(small) + 3 + len(pairs),)))

    def body(*refs):
        first_kernel(pairs, *refs)

    return pl.pallas_call(
        body,
        in_specs=[pl.BlockSpec(memory_space=pl.ANY)] * (2 + len(small)),
        out_specs=[held_whole()] * len(out_shape),
        out_shape=out_shape,
        scratch_shapes=scratch,
        compiler_params=params(FIRST_VMEM[pairs[0]]),
        cost_estimate=cost(2 * K * K * LON * 2 * len(pairs), 4 * K * LON * 2 * len(pairs)),
        name=f"first_source_{pairs[0]}",
    )(x, jacobian, *small)


def sweep_rows(north, table_ref, courant_ref, pass_rows, emit):
    halves = (slice(0, 128), slice(128, 256))
    lane = lax.broadcasted_iota(jnp.int32, (16, 128), 1)
    for quad in (0, 1) if north else (2, 3):
        east = quad in (0, 3)
        last = lane == 127 if east else lane == 0
        shift = 127 if east else 1
        order = halves if east else halves[::-1]

        def chunk(i, carry, quad=quad, last=last, shift=shift, order=order):
            d = quad * (QUAD // FREQ) + i // 2
            rows = pl.ds(pl.multiple_of((quad % 2) * QUAD + i * 16, 16), 16)
            speed = courant_ref[pl.ds(pl.multiple_of((i % 2) * 16, 16), 16), :]
            across = speed * table_ref[0, d]
            upward = speed * table_ref[1, d]
            centre = 1.0 - across - upward
            upward = upward / centre
            across = across / centre
            walled = jnp.where(last, 0.0, across)
            square = centre * centre

            def advance(v, first):
                turned = [
                    [pltpu.roll(value.astype(jnp.bfloat16), shift, 1).astype(jnp.float32) for value in half[:-1]]
                    for half in v
                ]
                fresh = [[], []]
                for t in range(len(v[0]) - 1):
                    beside = (jnp.where(last, turned[1][t], turned[0][t]), turned[1][t])
                    for half, weight in ((0, across), (1, walled)):
                        fresh[half].append(
                            pass_rows[first + t, :, order[half]]
                            * (v[half][t] + weight * beside[half] + upward * v[half][t + 1])
                        )
                return fresh

            emit(rows, order, advance, square * square)
            return carry

        lax.fori_loop(0, QUAD // 16, chunk, 0, unroll=3)


def own_passage(land_ref, clear_ref, pass_rows, north):
    passage = land_ref[...].astype(jnp.float32) * clear_ref[...]
    for t in range(ROWS):
        own = t if north else ROWS - 1 - t
        pass_rows[t] = jnp.broadcast_to(passage[own : own + 1, :], (16, LON))


def row_of(sources, r, *rest):
    for source in sources:
        if r < source.shape[0]:
            return source[(r, *rest)].astype(jnp.float32)
        r -= source.shape[0]


def inner_kernel(north, table_ref, land_ref, clear_ref, courant_ref, *rest):
    sources, (done, state, pass_rows) = rest[:-3], rest[-3:]
    own_passage(land_ref, clear_ref, pass_rows, north)

    def emit(rows, order, advance, scale):
        v = [[row_of(sources, t if north else ROWS - 1 - t, rows, lanes) for t in range(ROWS)] for lanes in order]
        for s in range(NSUB):
            v = advance(v, 0)
            if s < NSUB - 1:
                for half in range(2):
                    state[s, rows, order[half]] = v[half][-1]
        for half in range(2):
            for t in range(ROWS - NSUB):
                done[t if north else ROWS - NSUB - 1 - t, rows, order[half]] = (scale * v[half][t]).astype(jnp.bfloat16)

    sweep_rows(north, table_ref, courant_ref, pass_rows, emit)


def inner_sweep(north, table, land, clear, courant, sources):
    def body(*refs):
        inner_kernel(north, *refs)

    return pl.pallas_call(
        body,
        in_specs=[smem()] + [held_whole()] * (3 + len(sources)),
        out_specs=[held_whole()] * 2,
        out_shape=[
            jax.ShapeDtypeStruct((6, HALF, LON), jnp.bfloat16),
            jax.ShapeDtypeStruct((3, HALF, LON), jnp.float32),
        ],
        scratch_shapes=[pltpu.VMEM((ROWS, 16, LON), jnp.float32)],
        compiler_params=params(),
        cost_estimate=cost(30 * 7 * K * LON * 40, 60 * K * LON),
        name="inner_sweep_north" if north else "inner_sweep_south",
    )(table, land, clear, courant, *sources)


def outer_kernel(north, begin, count, messages, table_ref, land_ref, clear_ref, courant_ref, first, state, *rest):
    halo, done, pass_rows = rest[:messages], rest[messages], rest[-1]
    state_out = rest[messages + 1] if begin + count < HALO else None

    def halo_row(t, rows, lanes=slice(None)):
        place = (t // 2, t % 2 if north else 1 - t % 2)
        return halo[place[0]][place[1], rows, lanes].astype(jnp.float32)

    own_passage(land_ref, clear_ref, pass_rows, north)
    for t in range(begin + count):
        pieces = halo_row(t, slice(HALF, HALF + TAIL))
        pass_rows[ROWS + t] = jnp.broadcast_to(pieces[0:1] + pieces[1:2] + pieces[2:3], (16, LON))

    def emit(rows, order, advance, scale):
        v = []
        for lanes in order:
            if begin == 0:
                before = first[1 if north else 0, rows, lanes].astype(jnp.float32)
            else:
                before = halo_row(begin - 1, rows, lanes)
            v.append([before] + [halo_row(begin + t, rows, lanes) for t in range(count)])
        for s in range(NSUB):
            v = advance(v, ROWS - 1 + begin - s)
            if s < NSUB - 1:
                if state_out is not None:
                    for half in range(2):
                        state_out[s, rows, order[half]] = v[half][-1]
                v = [[state[s, rows, lanes]] + half for lanes, half in zip(order, v)]
        for half in range(2):
            for t in range(count):
                done[t if north else count - 1 - t, rows, order[half]] = (scale * v[half][t]).astype(jnp.bfloat16)

    sweep_rows(north, table_ref, courant_ref, pass_rows, emit)


def outer_sweep(north, begin, count, table, land, clear, courant, first, state, halos):
    def body(*refs):
        outer_kernel(north, begin, count, len(halos), *refs)

    out_shape = [jax.ShapeDtypeStruct((count, HALF, LON), jnp.bfloat16)]
    if begin + count < HALO:
        out_shape.append(jax.ShapeDtypeStruct((3, HALF, LON), jnp.float32))
    return pl.pallas_call(
        body,
        in_specs=[smem()] + [held_whole()] * (5 + len(halos)),
        out_specs=[held_whole()] * len(out_shape),
        out_shape=out_shape,
        scratch_shapes=[pltpu.VMEM((ROWS + HALO, 16, LON), jnp.float32)],
        compiler_params=params(),
        cost_estimate=cost(count * 4 * 7 * K * LON * 40, 50 * K * LON),
        name=f"outer_sweep_{'north' if north else 'south'}_{begin}",
    )(table, land, clear, courant, first, state, *halos)


def second_kernel(jobs, count, *refs):
    sources, refs = refs[:count], refs[count:]
    depth_ref, damp_ref, scale_ref, fd_ref, jac_ref, wave_ref = refs[:6]
    out_ref, wind_ref, held = refs[-3:]

    def run(pair, south_at, wind_at):
        north_at = (0, 2 * pair) if pair < 3 else (1, 2 * pair - 6)
        here = slice(2 * pair, 2 * pair + 2)
        depth = depth_ref[here, :]
        rate = jnp.zeros((2, LON), jnp.float32)
        for c in range(NCLASS):
            rate = jnp.where(depth == c, scale_ref[c], rate)
        damp = damp_ref[here, :]
        for half, (source, at) in enumerate((north_at, south_at)):
            for d in range(18):
                for piece in range(4):
                    e, side = divmod(piece, 2)
                    held[piece, pl.ds(half * 18 + d, FREQ, stride=DIR), :] = sources[source][
                        at + e, d * FREQ : (d + 1) * FREQ, side * 128 : (side + 1) * 128
                    ].astype(jnp.float32)
        spectrum = jnp.concatenate([held[piece].astype(jnp.bfloat16) for piece in range(4)], axis=1)
        for m in range(3):
            rows = slice(m * 384, (m + 1) * 384)
            mixed = contract(jac_ref[:, rows], spectrum)
            fd = fd_ref[rows, :]
            for piece in range(4):
                e, side = divmod(piece, 2)
                lanes = slice(side * 128, (side + 1) * 128)
                at = slice(piece * 128, (piece + 1) * 128)
                v = held[piece, rows, :]
                out_ref[e, rows, lanes] = (
                    v + rate[e : e + 1, lanes] * mixed[:, at] - (damp[e : e + 1, lanes] * fd) * v
                ).astype(jnp.bfloat16)
        wind = contract(wave_ref[...], spectrum)
        wind = wind[0:8] + wind[8:16] + wind[16:24]
        for e in range(2):
            wind_ref[e] = (sources[wind_at][e] + wind[:, e * LON : (e + 1) * LON])[:2]

    step = pl.program_id(0)
    for i, job in enumerate(jobs):
        pl.when(step == i)(lambda job=job: run(*job))


def second_source(jobs, sources, before, depth, damping, scale, fd, jac, wave):
    start = jobs[0][0]

    def body(*refs):
        second_kernel(jobs, len(sources), *refs)

    return pl.pallas_call(
        body,
        grid=(len(jobs),),
        in_specs=[held_whole()] * (len(sources) + 2)
        + [smem()]
        + [held_whole()] * 3
        + [pl.BlockSpec(memory_space=pl.ANY)] * len(before),
        out_specs=[
            pl.BlockSpec((2, K, LON), lambda i: (i + start, 0, 0)),
            pl.BlockSpec((2, 2, LON), lambda i: (i + start, 0, 0)),
        ],
        out_shape=[
            jax.ShapeDtypeStruct((ROWS, K, LON), jnp.bfloat16),
            jax.ShapeDtypeStruct((ROWS, 2, LON), jnp.float32),
        ],
        input_output_aliases={len(sources) + 6: 0, len(sources) + 7: 1} if before else {},
        scratch_shapes=[pltpu.VMEM((4, K, 128), jnp.float32)],
        compiler_params=params(),
        cost_estimate=cost(2 * K * K * LON * 2 * len(jobs), 4 * K * LON * 2 * len(jobs)),
        name=f"second_source_{start}",
    )(*sources, depth, damping, scale, fd, jac, wave, *before)


def body(
    adjoint_in,
    land_sea,
    depth_class,
    damping,
    transparency,
    outlets,
    flux_weight,
    jacobian,
    source_scale,
    freq_damp,
    courant,
    wind_growth,
):
    devices = lax.axis_size(AXES)
    x = adjoint_in.transpose(1, 0, 2)
    compass = np.zeros((K, 128), np.float32)
    for at in range(3):
        compass[:, 8 * at] = np.tile(np.cos(ANGLES), FREQ)
        compass[:, 8 * at + 1] = np.tile(np.sin(ANGLES), FREQ)
    comps = (flux_weight, freq_damp, wind_growth, jnp.asarray(compass))
    common = (land_sea, depth_class, damping, transparency, outlets, source_scale)
    down = [(i + 1, i) for i in range(devices - 1)]
    up = [(i, i + 1) for i in range(devices - 1)]
    speed = jnp.broadcast_to(courant[:, None], (FREQ, 128))
    table = jnp.asarray(np.abs(np.stack([np.cos(ANGLES), np.sin(ANGLES)])), jnp.float32)
    local = (table, land_sea, transparency, speed)
    n, s, winds, halo_s = {}, {}, {}, {}

    fw, fd, wave, n[0], s[0], winds[0] = first_source((0,), x, jacobian, *common, comps)
    halo_n = [lax.ppermute(n[0], AXES, down)]
    comps = (fw, fd, wave)
    n[1], s[1], winds[1] = first_source((1,), x, jacobian, *common, comps)
    halo_n.append(lax.ppermute(n[1], AXES, down))
    rest = (4, 3, 2)
    parts = first_source(rest, x, jacobian, *common, comps)
    for i, pair in enumerate(rest):
        n[pair], s[pair], winds[pair] = parts[3 * i : 3 * i + 3]
    in_s, state_s = inner_sweep(False, *local, [s[pair] for pair in range(5)])
    s[4], state_s, n[2] = lax.optimization_barrier((s[4], state_s, n[2]))
    halo_s[0] = lax.ppermute(s[4], AXES, up)
    in_n, state_n = inner_sweep(True, *local, [n[pair] for pair in range(5)])
    s[3], state_n = lax.optimization_barrier((s[3], state_n))
    halo_s[1] = lax.ppermute(s[3], AXES, up)
    last = (depth_class, damping, source_scale, fd, jacobian, wave)
    (edge,) = outer_sweep(True, 0, HALO, *local, n[4], state_n, halo_n)
    jobs = ((2, (2, 0), 3), (3, (2, 2), 4), (4, (2, 4), 5))
    part = second_source(jobs, (in_n, edge, in_s, winds[2], winds[3], winds[4]), (), *last)
    state_s, *part = lax.optimization_barrier((state_s, *part))
    edge, state_s = outer_sweep(False, 0, 2, *local, s[0], state_s, (halo_s[0],))
    part = second_source(((1, (1, 0), 2),), (in_n, edge, winds[1]), part, *last)
    state_s, *part = lax.optimization_barrier((state_s, *part))
    (edge,) = outer_sweep(False, 2, 2, *local, s[0], state_s, (halo_s[0], halo_s[1]))
    out, wind_out = second_source(((0, (1, 0), 2),), (in_n, edge, winds[0]), part, *last)
    return out.transpose(1, 0, 2), wind_out.transpose(1, 0, 2)


def solution(mesh):
    rows = P(AXES, None)
    placed = (P(None, AXES, None), rows, rows, rows, rows, P(), P(), P(), P(), P(), P(), P())
    return jax.shard_map(
        body,
        mesh=mesh,
        in_specs=placed,
        out_specs=(P(None, AXES, None), P(None, AXES, None)),
        check_vma=False,
    )
```

```python
import math

import jax
import jax.numpy as jnp
import numpy as np
from jax import lax
from jax.experimental import pallas as pl
from jax.experimental.pallas import tpu as pltpu
from jax.sharding import PartitionSpec as P

DIR = 36
FREQ = 32
NSUB = 4
NCLASS = 8
LON = 256
K = DIR * FREQ
HALF = K // 2
QUAD = K // 4
ROWS = 10
HALO = NSUB
TAIL = 16
AXES = ("pts", "grp")
VMEM = 28 * 1024 * 1024
FIRST_VMEM = {0: 57 * 1024 * 1024, 1: 54 * 1024 * 1024, 4: 28 * 1024 * 1024}

ANGLES = 2.0 * math.pi * (np.arange(DIR) + 0.5) / DIR


def params(limit=VMEM):
    return pltpu.CompilerParams(vmem_limit_bytes=limit)


def held_whole():
    return pl.BlockSpec(memory_space=pltpu.VMEM)


def smem():
    return pl.BlockSpec(memory_space=pltpu.SMEM)


def cost(flops, read):
    return pl.CostEstimate(flops=int(flops), bytes_accessed=int(read), transcendentals=0)


def three_pieces(x):
    hi = x.astype(jnp.bfloat16).astype(jnp.float32)
    mid = (x - hi).astype(jnp.bfloat16).astype(jnp.float32)
    return hi, mid, x - hi - mid


def stack_pieces(pieces):
    which = lax.broadcasted_iota(jnp.int32, (8, LON), 0)
    rows = jnp.zeros((8, LON), jnp.float32)
    for at, piece in enumerate(pieces):
        rows = jnp.where(which == at, jnp.broadcast_to(piece, (8, LON)), rows)
    return jnp.concatenate([rows, jnp.zeros((8, LON), jnp.float32)], axis=0).astype(jnp.bfloat16)


def contract(matrix, spectrum):
    return lax.dot_general(matrix, spectrum, (((0,), (0,)), ((), ())), preferred_element_type=jnp.float32)


def column(vector):
    return jnp.broadcast_to(vector[None, :], (128, K)).T


def point_fields(land_ref, depth_ref, outlets_ref, scale_ref, sea, count, rate):
    sea[...] = land_ref[...].astype(jnp.float32)
    depth = depth_ref[...]
    total = jnp.zeros((ROWS, LON), jnp.float32)
    for c in range(NCLASS):
        total = jnp.where(depth == c, scale_ref[c], total)
    rate[...] = total
    shape = (ROWS, LON)
    flat = lax.broadcasted_iota(jnp.int32, shape, 0) * LON + lax.broadcasted_iota(jnp.int32, shape, 1)
    flat = flat + lax.axis_index(AXES) * (ROWS * LON)
    hits = jnp.zeros(shape, jnp.float32)
    for n in range(outlets_ref.shape[0]):
        hits = hits + jnp.where(flat == outlets_ref[n], 1.0, 0.0)
    count[...] = hits


def first_kernel(pairs, x_ref, jac_hbm, *refs):
    opening = pairs[0] == 0
    tables = 4 if opening else 3
    far = refs[: 6 + tables]
    outs = refs[6 + tables : -7 - len(far)]
    sea, count, rate, held, x_near, jac_ref = refs[-7 - len(far) : -1 - len(far)]
    near, sems = refs[-1 - len(far) : -1], refs[-1]
    copies = [pltpu.make_async_copy(a, b, sems.at[i]) for i, (a, b) in enumerate(zip(far, near))]
    waits = [pltpu.make_async_copy(jac_hbm, jac_ref, sems.at[len(far)])]
    for i, pair in enumerate(pairs):
        waits.append(
            pltpu.make_async_copy(
                x_ref.at[2 * pair : 2 * pair + 2], x_near.at[2 * i : 2 * i + 2], sems.at[len(far) + 1 + i]
            )
        )
    for copy in copies + waits:
        copy.start()
    for copy in copies:
        copy.wait()
    land_ref, depth_ref, damp_ref, clear_ref, outlets_ref, scale_ref = near[:6]
    if opening:
        weight_ref, freq_ref, growth_ref, compass_ref = near[6:]
        fw_ref, fd_ref, wave_ref = outs[:3]
        outs = outs[3:]
        fw_ref[...] = column(weight_ref[...])
        fd_ref[...] = column(freq_ref[...])
        hi, mid, low = three_pieces(column(growth_ref[...]) * compass_ref[...])
        lane = lax.broadcasted_iota(jnp.int32, (K, 128), 1)
        wave_ref[...] = jnp.where(lane < 8, hi, jnp.where(lane < 16, mid, low)).astype(jnp.bfloat16)
    else:
        fw_ref, fd_ref, wave_ref = near[6:]
    point_fields(land_ref, depth_ref, outlets_ref, scale_ref, sea, count, rate)

    for i, pair in enumerate(pairs):
        waits[1 + i].wait()
        to = 2 * i if opening else 0
        halves, wind_ref = (outs[:2], outs[2]) if opening else (outs[3 * i : 3 * i + 2], outs[3 * i + 2])
        fw = fw_ref[...]
        fw = jnp.concatenate([fw, fw], axis=1)
        seeds = []
        fields = []
        for e in range(2):
            r = slice(2 * pair + e, 2 * pair + e + 1)
            lone = sea[r, :] * (x_near[2 * i + e].astype(jnp.float32) + fw * count[r, :])
            seeds.append(lone.astype(jnp.bfloat16))
            fields.append((rate[r, :], damp_ref[r, :]))
        spectrum = jnp.concatenate(seeds, axis=1)
        if i == 0:
            waits[0].wait()
        for m in range(3):
            rows = slice(m * 384, (m + 1) * 384)
            mixed = contract(jac_ref[:, rows], spectrum)
            fd = fd_ref[rows, :]
            for piece in range(4):
                e, side = divmod(piece, 2)
                lanes = slice(side * 128, (side + 1) * 128)
                at = slice(piece * 128, (piece + 1) * 128)
                v = seeds[e][rows, lanes].astype(jnp.float32)
                held[piece, rows, :] = (
                    v + fields[e][0][:, lanes] * mixed[:, at] - (fields[e][1][:, lanes] * fd) * v
                )
        wind = contract(wave_ref[...], spectrum)
        wind = wind[0:8] + wind[8:16] + wind[16:24]
        for e in range(2):
            wind_ref[to + e] = wind[:, e * LON : (e + 1) * LON]
        for half in range(2):
            for d in range(18):
                for piece in range(4):
                    e, side = divmod(piece, 2)
                    halves[half][to + e, d * FREQ : (d + 1) * FREQ, side * 128 : (side + 1) * 128] = held[
                        piece, pl.ds(half * 18 + d, FREQ, stride=DIR), :
                    ].astype(jnp.bfloat16)
        if pair != 2:
            for e in range(2):
                r = slice(2 * pair + e, 2 * pair + e + 1)
                pieces = three_pieces(sea[r, :] * clear_ref[r, :])
                halves[0 if pair < 2 else 1][to + e, HALF : HALF + TAIL, :] = stack_pieces(pieces)


def first_source(pairs, x, jacobian, land, depth, damping, clear, outlets, scale, comps):
    out_shape = []
    if pairs[0] == 0:
        out_shape += [jax.ShapeDtypeStruct((K, 128), dtype) for dtype in (jnp.float32, jnp.float32, jnp.bfloat16)]
    for pair in pairs[:1] if pairs[0] == 0 else pairs:
        count_rows = 2 * len(pairs) if pairs[0] == 0 else 2
        for size in (HALF + TAIL if pair < 2 else HALF, HALF + TAIL if pair > 2 else HALF):
            out_shape.append(jax.ShapeDtypeStruct((count_rows, size, LON), jnp.bfloat16))
        out_shape.append(jax.ShapeDtypeStruct((count_rows, 8, LON), jnp.float32))
    small = (land, depth, damping, clear, outlets, scale, *comps)
    scratch = [pltpu.VMEM((ROWS, LON), jnp.float32)] * 3 + [pltpu.VMEM((4, K, 128), jnp.float32)]
    scratch += [pltpu.VMEM((2 * len(pairs), K, LON), jnp.bfloat16), pltpu.VMEM((K, K), jnp.bfloat16)]
    for at, a in enumerate(small):
        scratch.append((pltpu.SMEM if at in (4, 5) else pltpu.VMEM)(a.shape, a.dtype))
    scratch.append(pltpu.SemaphoreType.DMA((len(small) + 1 + len(pairs),)))

    def body(*refs):
        first_kernel(pairs, *refs)

    return pl.pallas_call(
        body,
        in_specs=[pl.BlockSpec(memory_space=pl.ANY)] * (2 + len(small)),
        out_specs=[held_whole()] * len(out_shape),
        out_shape=out_shape,
        scratch_shapes=scratch,
        compiler_params=params(FIRST_VMEM[pairs[0]]),
        cost_estimate=cost(2 * K * K * LON * 2 * len(pairs), 4 * K * LON * 2 * len(pairs)),
        name=f"first_source_{pairs[0]}",
    )(x, jacobian, *small)


def sweep_rows(north, table_ref, courant_ref, pass_rows, emit):
    halves = (slice(0, 128), slice(128, 256))
    lane = lax.broadcasted_iota(jnp.int32, (16, 128), 1)
    for quad in (0, 1) if north else (2, 3):
        east = quad in (0, 3)
        last = lane == 127 if east else lane == 0
        shift = 127 if east else 1
        order = halves if east else halves[::-1]

        def chunk(i, carry, quad=quad, last=last, shift=shift, order=order):
            d = quad * (QUAD // FREQ) + i // 2
            rows = pl.ds(pl.multiple_of((quad % 2) * QUAD + i * 16, 16), 16)
            speed = courant_ref[pl.ds(pl.multiple_of((i % 2) * 16, 16), 16), :]
            across = speed * table_ref[0, d]
            upward = speed * table_ref[1, d]
            centre = 1.0 - across - upward
            upward = upward / centre
            across = across / centre
            walled = jnp.where(last, 0.0, across)
            square = centre * centre

            def advance(v, first):
                turned = [
                    [pltpu.roll(value.astype(jnp.bfloat16), shift, 1).astype(jnp.float32) for value in half[:-1]]
                    for half in v
                ]
                fresh = [[], []]
                for t in range(len(v[0]) - 1):
                    beside = (jnp.where(last, turned[1][t], turned[0][t]), turned[1][t])
                    for half, weight in ((0, across), (1, walled)):
                        fresh[half].append(
                            pass_rows[first + t, :, order[half]]
                            * (v[half][t] + weight * beside[half] + upward * v[half][t + 1])
                        )
                return fresh

            emit(rows, order, advance, square * square)
            return carry

        lax.fori_loop(0, QUAD // 16, chunk, 0, unroll=3)


def own_passage(land_ref, clear_ref, pass_rows, north):
    passage = land_ref[...].astype(jnp.float32) * clear_ref[...]
    for t in range(ROWS):
        own = t if north else ROWS - 1 - t
        pass_rows[t] = jnp.broadcast_to(passage[own : own + 1, :], (16, LON))


def row_of(sources, r, *rest):
    for source in sources:
        if r < source.shape[0]:
            return source[(r, *rest)].astype(jnp.float32)
        r -= source.shape[0]


def inner_kernel(north, table_ref, land_ref, clear_ref, courant_ref, *rest):
    sources, (done, state, pass_rows) = rest[:-3], rest[-3:]
    own_passage(land_ref, clear_ref, pass_rows, north)

    def emit(rows, order, advance, scale):
        v = [[row_of(sources, t if north else ROWS - 1 - t, rows, lanes) for t in range(ROWS)] for lanes in order]
        for s in range(NSUB):
            v = advance(v, 0)
            if s < NSUB - 1:
                for half in range(2):
                    state[s, rows, order[half]] = v[half][-1]
        for half in range(2):
            for t in range(ROWS - NSUB):
                done[t if north else ROWS - NSUB - 1 - t, rows, order[half]] = (scale * v[half][t]).astype(jnp.bfloat16)

    sweep_rows(north, table_ref, courant_ref, pass_rows, emit)


def inner_sweep(north, table, land, clear, courant, sources):
    def body(*refs):
        inner_kernel(north, *refs)

    return pl.pallas_call(
        body,
        in_specs=[smem()] + [held_whole()] * (3 + len(sources)),
        out_specs=[held_whole()] * 2,
        out_shape=[
            jax.ShapeDtypeStruct((6, HALF, LON), jnp.bfloat16),
            jax.ShapeDtypeStruct((3, HALF, LON), jnp.float32),
        ],
        scratch_shapes=[pltpu.VMEM((ROWS, 16, LON), jnp.float32)],
        compiler_params=params(),
        cost_estimate=cost(30 * 7 * K * LON * 40, 60 * K * LON),
        name="inner_sweep_north" if north else "inner_sweep_south",
    )(table, land, clear, courant, *sources)


def outer_kernel(north, begin, count, messages, table_ref, land_ref, clear_ref, courant_ref, first, state, *rest):
    halo, done, pass_rows = rest[:messages], rest[messages], rest[-1]
    state_out = rest[messages + 1] if begin + count < HALO else None

    def halo_row(t, rows, lanes=slice(None)):
        place = (t // 2, t % 2 if north else 1 - t % 2)
        return halo[place[0]][place[1], rows, lanes].astype(jnp.float32)

    own_passage(land_ref, clear_ref, pass_rows, north)
    for t in range(begin + count):
        pieces = halo_row(t, slice(HALF, HALF + TAIL))
        pass_rows[ROWS + t] = jnp.broadcast_to(pieces[0:1] + pieces[1:2] + pieces[2:3], (16, LON))

    def emit(rows, order, advance, scale):
        v = []
        for lanes in order:
            if begin == 0:
                before = first[1 if north else 0, rows, lanes].astype(jnp.float32)
            else:
                before = halo_row(begin - 1, rows, lanes)
            v.append([before] + [halo_row(begin + t, rows, lanes) for t in range(count)])
        for s in range(NSUB):
            v = advance(v, ROWS - 1 + begin - s)
            if s < NSUB - 1:
                if state_out is not None:
                    for half in range(2):
                        state_out[s, rows, order[half]] = v[half][-1]
                v = [[state[s, rows, lanes]] + half for lanes, half in zip(order, v)]
        for half in range(2):
            for t in range(count):
                done[t if north else count - 1 - t, rows, order[half]] = (scale * v[half][t]).astype(jnp.bfloat16)

    sweep_rows(north, table_ref, courant_ref, pass_rows, emit)


def outer_sweep(north, begin, count, table, land, clear, courant, first, state, halos):
    def body(*refs):
        outer_kernel(north, begin, count, len(halos), *refs)

    out_shape = [jax.ShapeDtypeStruct((count, HALF, LON), jnp.bfloat16)]
    if begin + count < HALO:
        out_shape.append(jax.ShapeDtypeStruct((3, HALF, LON), jnp.float32))
    return pl.pallas_call(
        body,
        in_specs=[smem()] + [held_whole()] * (5 + len(halos)),
        out_specs=[held_whole()] * len(out_shape),
        out_shape=out_shape,
        scratch_shapes=[pltpu.VMEM((ROWS + HALO, 16, LON), jnp.float32)],
        compiler_params=params(),
        cost_estimate=cost(count * 4 * 7 * K * LON * 40, 50 * K * LON),
        name=f"outer_sweep_{'north' if north else 'south'}_{begin}",
    )(table, land, clear, courant, first, state, *halos)


def second_kernel(jobs, count, *refs):
    sources, refs = refs[:count], refs[count:]
    depth_ref, damp_ref, scale_ref, fd_ref, jac_ref, wave_ref = refs[:6]
    out_ref, wind_ref, held = refs[-3:]

    def run(pair, south_at, wind_at):
        north_at = (0, 2 * pair) if pair < 3 else (1, 2 * pair - 6)
        here = slice(2 * pair, 2 * pair + 2)
        depth = depth_ref[here, :]
        rate = jnp.zeros((2, LON), jnp.float32)
        for c in range(NCLASS):
            rate = jnp.where(depth == c, scale_ref[c], rate)
        damp = damp_ref[here, :]
        for half, (source, at) in enumerate((north_at, south_at)):
            for d in range(18):
                for piece in range(4):
                    e, side = divmod(piece, 2)
                    held[piece, pl.ds(half * 18 + d, FREQ, stride=DIR), :] = sources[source][
                        at + e, d * FREQ : (d + 1) * FREQ, side * 128 : (side + 1) * 128
                    ].astype(jnp.float32)
        spectrum = jnp.concatenate([held[piece].astype(jnp.bfloat16) for piece in range(4)], axis=1)
        for m in range(3):
            rows = slice(m * 384, (m + 1) * 384)
            mixed = contract(jac_ref[:, rows], spectrum)
            fd = fd_ref[rows, :]
            for piece in range(4):
                e, side = divmod(piece, 2)
                lanes = slice(side * 128, (side + 1) * 128)
                at = slice(piece * 128, (piece + 1) * 128)
                v = held[piece, rows, :]
                out_ref[e, rows, lanes] = (
                    v + rate[e : e + 1, lanes] * mixed[:, at] - (damp[e : e + 1, lanes] * fd) * v
                ).astype(jnp.bfloat16)
        wind = contract(wave_ref[...], spectrum)
        wind = wind[0:8] + wind[8:16] + wind[16:24]
        for e in range(2):
            wind_ref[e] = (sources[wind_at][e] + wind[:, e * LON : (e + 1) * LON])[:2]

    step = pl.program_id(0)
    for i, job in enumerate(jobs):
        pl.when(step == i)(lambda job=job: run(*job))


def second_source(jobs, sources, before, depth, damping, scale, fd, jac, wave):
    start = jobs[0][0]

    def body(*refs):
        second_kernel(jobs, len(sources), *refs)

    return pl.pallas_call(
        body,
        grid=(len(jobs),),
        in_specs=[held_whole()] * (len(sources) + 2)
        + [smem()]
        + [held_whole()] * 3
        + [pl.BlockSpec(memory_space=pl.ANY)] * len(before),
        out_specs=[
            pl.BlockSpec((2, K, LON), lambda i: (i + start, 0, 0)),
            pl.BlockSpec((2, 2, LON), lambda i: (i + start, 0, 0)),
        ],
        out_shape=[
            jax.ShapeDtypeStruct((ROWS, K, LON), jnp.bfloat16),
            jax.ShapeDtypeStruct((ROWS, 2, LON), jnp.float32),
        ],
        input_output_aliases={len(sources) + 6: 0, len(sources) + 7: 1} if before else {},
        scratch_shapes=[pltpu.VMEM((4, K, 128), jnp.float32)],
        compiler_params=params(),
        cost_estimate=cost(2 * K * K * LON * 2 * len(jobs), 4 * K * LON * 2 * len(jobs)),
        name=f"second_source_{start}",
    )(*sources, depth, damping, scale, fd, jac, wave, *before)


def body(
    adjoint_in,
    land_sea,
    depth_class,
    damping,
    transparency,
    outlets,
    flux_weight,
    jacobian,
    source_scale,
    freq_damp,
    courant,
    wind_growth,
):
    devices = lax.axis_size(AXES)
    x = adjoint_in.transpose(1, 0, 2)
    compass = np.zeros((K, 128), np.float32)
    for at in range(3):
        compass[:, 8 * at] = np.tile(np.cos(ANGLES), FREQ)
        compass[:, 8 * at + 1] = np.tile(np.sin(ANGLES), FREQ)
    comps = (flux_weight, freq_damp, wind_growth, jnp.asarray(compass))
    common = (land_sea, depth_class, damping, transparency, outlets, source_scale)
    down = [(i + 1, i) for i in range(devices - 1)]
    up = [(i, i + 1) for i in range(devices - 1)]
    speed = jnp.broadcast_to(courant[:, None], (FREQ, 128))
    table = jnp.asarray(np.abs(np.stack([np.cos(ANGLES), np.sin(ANGLES)])), jnp.float32)
    local = (table, land_sea, transparency, speed)
    n, s, winds, halo_s = {}, {}, {}, {}

    fw, fd, wave, n[0], s[0], winds[0] = first_source((0,), x, jacobian, *common, comps)
    halo_n = [lax.ppermute(n[0], AXES, down)]
    comps = (fw, fd, wave)
    n[1], s[1], winds[1] = first_source((1,), x, jacobian, *common, comps)
    halo_n.append(lax.ppermute(n[1], AXES, down))
    rest = (4, 3, 2)
    parts = first_source(rest, x, jacobian, *common, comps)
    for i, pair in enumerate(rest):
        n[pair], s[pair], winds[pair] = parts[3 * i : 3 * i + 3]
    in_s, state_s = inner_sweep(False, *local, [s[pair] for pair in range(5)])
    s[4], state_s, n[2] = lax.optimization_barrier((s[4], state_s, n[2]))
    halo_s[0] = lax.ppermute(s[4], AXES, up)
    in_n, state_n = inner_sweep(True, *local, [n[pair] for pair in range(5)])
    s[3], state_n = lax.optimization_barrier((s[3], state_n))
    halo_s[1] = lax.ppermute(s[3], AXES, up)
    last = (depth_class, damping, source_scale, fd, jacobian, wave)
    (edge,) = outer_sweep(True, 0, HALO, *local, n[4], state_n, halo_n)
    jobs = ((2, (2, 0), 3), (3, (2, 2), 4), (4, (2, 4), 5))
    part = second_source(jobs, (in_n, edge, in_s, winds[2], winds[3], winds[4]), (), *last)
    state_s, *part = lax.optimization_barrier((state_s, *part))
    edge, state_s = outer_sweep(False, 0, 2, *local, s[0], state_s, (halo_s[0],))
    part = second_source(((1, (1, 0), 2),), (in_n, edge, winds[1]), part, *last)
    state_s, *part = lax.optimization_barrier((state_s, *part))
    (edge,) = outer_sweep(False, 2, 2, *local, s[0], state_s, (halo_s[0], halo_s[1]))
    out, wind_out = second_source(((0, (1, 0), 2),), (in_n, edge, winds[0]), part, *last)
    return out.transpose(1, 0, 2), wind_out.transpose(1, 0, 2)


def solution(mesh):
    rows = P(AXES, None)
    placed = (P(None, AXES, None), rows, rows, rows, rows, P(), P(), P(), P(), P(), P(), P())
    return jax.shard_map(
        body,
        mesh=mesh,
        in_specs=placed,
        out_specs=(P(None, AXES, None), P(None, AXES, None)),
        check_vma=False,
    )
```
